512 devices in a mesh: blk: 32 (over z, core), grp: 16 (over x, y).
Axes of the slice: x: 4, y: 4, z: 16, core: 2. Of those that a mesh axis runs over, the one named last changes fastest.
Arguments:
- signal: bfloat16 [16, 64, 16384], P('grp', None, 'blk'), may hold values from -10 to 10
- lag_table: int32 [512], replicated, may hold values from 0 to 511, each once
- window_end: int32 [16, 32], P('grp', 'blk'), may hold values from 128 to 512
Outputs:
- factors: float32 [16, 512, 512], P('grp', 'blk')
- coeffs: float32 [16, 512, 64], P('grp', 'blk')
- residual: float32 [16, 64, 16384], P('grp', None, 'blk')
The draws below stay inside these ranges and needn't reach their ends.
Inputs may be any that keep to these rules, and one draw needn't show every extreme that they name: `lag_table`: each of 0 to 511 appears once.
All inputs are finite; a program needn't handle non-finite values.
Results may differ from the reference program's by a relative error of at most 0.0003.
Values may be sent and summed in bfloat16 or wider, within the bound.
No kernel may reach another device: no remote copies, remote signals or barrier semaphores. Data moves between devices by JAX's collectives and lax.ppermute only.
A program may use at most 192 MiB of HBM per device.

```python
import math
import jax
import jax.numpy as jnp
from jax import lax

SENSORS = 64
LAGS = 8
ROWS = 512
COLS = 512
NBLOCKS = 32
NGROUPS = 16
SPAN = 16384


period_steps = 64


def draw_signal(key, part):
    key_list = jax.random.split(key, 5)
    group_times = jnp.arange(NGROUPS, dtype=jnp.int32)[:, None] * SPAN + jnp.arange(SPAN, dtype=jnp.int32)[None, :]
    frequency = jax.random.randint(key_list[0], (SENSORS,), 1, period_steps // 2)
    turn_index = group_times[:, None, :] * frequency[None, :, None] % period_steps
    phases = jax.random.uniform(key_list[1], (SENSORS,), jnp.float32, -math.pi, math.pi)
    wave_part = 0.7 * jnp.sin(2.0 * math.pi * turn_index.astype(jnp.float32) / period_steps + phases[None, :, None])
    levels = jax.random.uniform(key_list[2], (NGROUPS, 1, NBLOCKS, 1), jnp.float32, 0.5, 1.5)
    noise_part = jnp.clip(jax.random.normal(key_list[3], (NGROUPS, SENSORS, NBLOCKS, ROWS), jnp.float32), -4.0, 4.0)
    scales = jax.random.uniform(key_list[4], (SENSORS,), jnp.float32, 0.7, 1.4)
    rough_part = (noise_part * levels).reshape(NGROUPS, SENSORS, SPAN)
    values = scales[None, :, None] * (wave_part + rough_part)
    return values.astype(jnp.bfloat16)


def draw_window_end(key, part):
    key_list = jax.random.split(key, 2)
    ends_flat = jax.random.randint(key_list[0], (NGROUPS * NBLOCKS,), ROWS // 4, ROWS + 1)
    positions = jax.random.permutation(key_list[1], NGROUPS * NBLOCKS)
    ends_flat = ends_flat.at[positions[0]].set(ROWS).at[positions[1]].set(ROWS // 4)
    return ends_flat.reshape(NGROUPS, NBLOCKS).astype(jnp.int32)


def setup_inputs(seed: int = 0) -> dict:
    splits = jax.random.split(jax.random.key(seed), 4)
    return {
        "signal": draw_signal(jax.random.fold_in(splits[3], 71), 0),
        "lag_table": jax.random.permutation(splits[1], COLS).astype(jnp.int32),
        "window_end": draw_window_end(jax.random.fold_in(splits[3], 71), 0),
    }


ridge_weight = 4.0

def lagged_block(history, row_start, block_len, lag_count):
    pieces = [lax.dynamic_slice_in_dim(history, row_start + (lag_count - 1 - delay_index), block_len, 1) for delay_index in range(lag_count)]
    return jnp.concatenate(pieces, axis=0)

def highest(first_matrix, second_matrix):
    return jnp.dot(first_matrix, second_matrix, precision=lax.Precision.HIGHEST)

def reference(signal, lag_table, window_end):
    block_len = min(512, ROWS)
    per_group = SPAN // block_len
    series = jnp.transpose(signal, (1, 0, 2)).reshape(SENSORS, NGROUPS * SPAN)
    padded = jnp.concatenate([jnp.zeros((SENSORS, LAGS), signal.dtype), series], axis=1)

    def group_history(group_index):
        return lax.dynamic_slice_in_dim(padded, (group_index * SPAN).astype(jnp.int32), SPAN + LAGS, 1)

    def group_terms(group_index):
        history = group_history(group_index)
        group_ends = window_end[group_index]

        def add_block(carry_pair, step_index):
            gram_part, cross_part = carry_pair
            row_start = (step_index * block_len).astype(jnp.int32)
            lagged = lagged_block(history, row_start, block_len, LAGS).astype(jnp.float32)
            target = lax.dynamic_slice_in_dim(history, row_start + LAGS, block_len, 1).astype(jnp.float32)
            device = row_start // ROWS
            local_rows = row_start % ROWS + jnp.arange(block_len, dtype=jnp.int32)
            live_mask = local_rows < group_ends[device]
            masked = jnp.where(live_mask[None, :], lagged, jnp.zeros_like(lagged))
            gram_part = gram_part + jnp.dot(masked.astype(jnp.float32), lagged.T.astype(jnp.float32), preferred_element_type=jnp.float32)
            cross_part = cross_part + jnp.dot(masked.astype(jnp.float32), target.T.astype(jnp.float32), preferred_element_type=jnp.float32)
            return ((gram_part, cross_part), None)
        start_gram = NBLOCKS * ridge_weight * jnp.eye(COLS, dtype=jnp.float32)
        start_cross = jnp.zeros((COLS, SENSORS), jnp.float32)
        sums_pair, unused = lax.scan(add_block, (start_gram, start_cross), jnp.arange(per_group, dtype=jnp.int32))
        return sums_pair
    grams, crosses = lax.map(group_terms, jnp.arange(NGROUPS, dtype=jnp.int32))
    prefix_grams = jnp.cumsum(grams, axis=0)
    prefix_crosses = jnp.cumsum(crosses, axis=0)

    def solve_group(sums_pair):
        gram_part, cross_part = sums_pair
        ordered = gram_part[lag_table][:, lag_table]
        lower_factor = jnp.linalg.cholesky(ordered)
        half_solved = lax.linalg.triangular_solve(lower_factor, cross_part[lag_table], left_side=True, lower=True)
        coefficients = lax.linalg.triangular_solve(lower_factor, half_solved, left_side=True, lower=True, transpose_a=True)
        return (lower_factor.T / math.sqrt(SPAN), coefficients)
    factors, coeffs = lax.map(solve_group, (prefix_grams, prefix_crosses))

    def group_residual(group_index):
        history = group_history(group_index)
        canonical = jnp.zeros((COLS, SENSORS), coeffs.dtype).at[lag_table].set(coeffs[group_index])

        def one_block(step_index):
            row_start = (step_index * block_len).astype(jnp.int32)
            lagged = lagged_block(history, row_start, block_len, LAGS).astype(jnp.float32)
            target = lax.dynamic_slice_in_dim(history, row_start + LAGS, block_len, 1).astype(jnp.float32)
            return target - highest(canonical.T, lagged)
        pieces = lax.map(one_block, jnp.arange(per_group, dtype=jnp.int32))
        return jnp.transpose(pieces, (1, 0, 2)).reshape(SENSORS, SPAN)
    residual = lax.map(group_residual, jnp.arange(NGROUPS, dtype=jnp.int32))
    return (factors, coeffs, residual)
```

```python
import jax
import jax.numpy as jnp
from jax import lax
from jax.experimental import pallas as pl
from jax.experimental.pallas import tpu as pltpu
from jax.sharding import PartitionSpec as P

F32 = jnp.float32
BF16 = jnp.bfloat16
RIDGE = 4.0
SENSORS = 64
LAGS = 8
COLS = 512
ROWS = 512
TILE = 128
NT = COLS // TILE
TILES = [(k, j) for k in range(NT) for j in range(k, NT)]
PACKED = (len(TILES) + NT // 2) * TILE
VMEM = pl.BlockSpec(memory_space=pltpu.VMEM)
SMEM = pl.BlockSpec(memory_space=pltpu.SMEM)


def dot(a, b, ca, cb, precision=None):
    return lax.dot_general(
        a, b, (((ca,), (cb,)), ((), ())), precision=precision, preferred_element_type=F32
    )


def gram_kernel(end_ref, table_ref, tail_ref, x_ref, lagged_ref, packed_ref):
    x = x_ref[...]
    ext = jnp.concatenate([tail_ref[...], x], axis=1).astype(F32)
    pieces = [pltpu.roll(ext, d, 1)[:, TILE:].astype(BF16) for d in range(1, LAGS + 1)]
    canonical = jnp.concatenate(pieces, axis=0)
    pair = lax.broadcasted_iota(jnp.int32, (COLS, COLS), 0)
    chosen = jnp.where(pair == table_ref[...], 1.0, 0.0).astype(BF16)
    lagged = dot(chosen, canonical, 0, 0).astype(BF16)
    lagged_ref[...] = lagged
    time = lax.broadcasted_iota(jnp.int32, (COLS, ROWS), 1)
    masked = jnp.where(time < end_ref[0, 0], lagged.astype(F32), 0.0).astype(BF16)
    eye = (
        lax.broadcasted_iota(jnp.int32, (TILE, TILE), 0)
        == lax.broadcasted_iota(jnp.int32, (TILE, TILE), 1)
    )
    ridge = jnp.where(eye, RIDGE, 0.0)
    n = 0
    for k in range(NT):
        rows = masked[k * TILE : (k + 1) * TILE]
        block = dot(rows, lagged[k * TILE :], 1, 1)
        for j in range(k, NT):
            tile = block[:, (j - k) * TILE : (j - k + 1) * TILE]
            packed_ref[n * TILE : (n + 1) * TILE, :] = tile + ridge if j == k else tile
            n += 1
    cross = dot(masked, x, 1, 1)
    half = COLS // 2
    packed_ref[n * TILE :, :] = jnp.concatenate([cross[:half], cross[half:]], axis=1)


def factor_tile(d_rows):
    n = len(d_rows)
    lane = lax.broadcasted_iota(jnp.int32, (8, TILE), 1)
    sub = lax.broadcasted_iota(jnp.int32, (8, TILE), 0)
    d = list(d_rows)
    x = [jnp.where(lane == 8 * q + sub, 1.0, 0.0) for q in range(n)]

    def col(v, c):
        return jnp.broadcast_to(v[:, c : c + 1], (8, TILE))

    def row(v, i):
        return jnp.broadcast_to(v[i : i + 1, :], (8, TILE))

    for p in range(n):
        base = 8 * p
        c = [col(d[p], base + j) for j in range(8)]
        s = {(i, j): row(c[j], i) for j in range(8) for i in range(j + 1)}
        r = [row(d[p], i) for i in range(8)]
        xr = [row(x[p], i) for i in range(8)]
        cn = [col(d[p + 1], base + j) for j in range(8)] if p + 1 < n else []
        u = {}
        inv = []
        for k in range(8):
            w = lax.rsqrt(s[k, k])
            inv.append(w)
            for j in range(k + 1, 8):
                u[k, j] = s[k, j] * w
            for i in range(k + 1, 8):
                for j in range(i, 8):
                    s[i, j] = s[i, j] - u[k, i] * u[k, j]
            r[k] = r[k] * w
            xr[k] = xr[k] * w
            if cn:
                cn[k] = cn[k] * w
            for i in range(k + 1, 8):
                r[i] = r[i] - u[k, i] * r[k]
                xr[i] = xr[i] - u[k, i] * xr[k]
                if cn:
                    cn[i] = cn[i] - u[k, i] * cn[k]
        if p + 1 < n:
            t = [cn[i] * r[i] for i in range(8)]
            d[p + 1] = d[p + 1] - (((t[0] + t[1]) + (t[2] + t[3])) + ((t[4] + t[5]) + (t[6] + t[7])))
            t = [cn[i] * xr[i] for i in range(8)]
            x[p + 1] = x[p + 1] - (((t[0] + t[1]) + (t[2] + t[3])) + ((t[4] + t[5]) + (t[6] + t[7])))
        if p + 2 < n:
            z = list(r)
            xz = list(xr)
            for k in reversed(range(8)):
                z[k] = z[k] * inv[k]
                xz[k] = xz[k] * inv[k]
                for i in range(k):
                    z[i] = z[i] - u[i, k] * z[k]
                    xz[i] = xz[i] - u[i, k] * xz[k]
            for q in range(p + 2, n):
                cq = [col(d[q], base + j) for j in range(8)]
                t = [cq[i] * z[i] for i in range(8)]
                d[q] = d[q] - (((t[0] + t[1]) + (t[2] + t[3])) + ((t[4] + t[5]) + (t[6] + t[7])))
                t = [cq[i] * xz[i] for i in range(8)]
                x[q] = x[q] - (((t[0] + t[1]) + (t[2] + t[3])) + ((t[4] + t[5]) + (t[6] + t[7])))
        du, dx = r[0], xr[0]
        for i in range(1, 8):
            du = jnp.where(sub == i, r[i], du)
            dx = jnp.where(sub == i, xr[i], dx)
        d[p] = jnp.where(lane >= base + sub, du, 0.0)
        x[p] = dx
    return d, x


def fit_kernel(blk_ref, packed_ref, lagged_ref, x_ref, factor_ref, coef_ref, resid_ref, u_ref, i_ref, w_ref):
    high = lax.Precision.HIGHEST
    half = COLS // 2
    tiles = {}
    for n, (k, j) in enumerate(TILES):
        tiles[k, j] = (n * TILE,)
    base = len(TILES) * TILE
    g = {kj: packed_ref[at : at + TILE, :] for kj, (at,) in tiles.items()}
    b = []
    for k in range(NT):
        at = base + (k * TILE) % half
        lo = (k * TILE // half) * SENSORS
        b.append(packed_ref[at : at + TILE, lo : lo + SENSORS])
    u_ref[...] = jnp.zeros_like(u_ref)
    y = []
    for k in range(NT):
        d, xi = factor_tile([g[k, k][8 * q : 8 * q + 8] for q in range(TILE // 8)])
        ukk = jnp.concatenate(d, axis=0)
        xkk = jnp.concatenate(xi, axis=0)
        i_ref[k * TILE : (k + 1) * TILE, :] = xkk
        u_ref[k * TILE : (k + 1) * TILE, k * TILE : (k + 1) * TILE] = ukk
        panel = {}
        for j in range(k + 1, NT):
            panel[j] = dot(xkk, g[k, j], 1, 0, high)
            u_ref[k * TILE : (k + 1) * TILE, j * TILE : (j + 1) * TILE] = panel[j]
        y.append(dot(xkk, b[k], 1, 0, high))
        for i in range(k + 1, NT):
            for j in range(i, NT):
                g[i, j] = g[i, j] - dot(panel[i], panel[j], 0, 0, high)
            b[i] = b[i] - dot(panel[i], y[k], 0, 0, high)
    w = [None] * NT
    for k in reversed(range(NT)):
        acc = y[k]
        for j in range(k + 1, NT):
            ukj = u_ref[k * TILE : (k + 1) * TILE, j * TILE : (j + 1) * TILE]
            acc = acc - dot(ukj, w[j], 1, 0, high)
        w[k] = dot(i_ref[k * TILE : (k + 1) * TILE, :], acc, 0, 0, high)
        w_ref[k * TILE : (k + 1) * TILE, :] = w[k]
    share = factor_ref.shape[0]
    first = pl.multiple_of(blk_ref[0, 0] * share, 8)
    factor_ref[...] = u_ref[pl.ds(first, share), :] * (1.0 / 128.0)
    coef_ref[...] = w_ref[pl.ds(first, share), :]
    wt = jnp.concatenate([w_ref[...], jnp.zeros((COLS, TILE - SENSORS), F32)], axis=1).T[:SENSORS]
    hi = wt.astype(BF16)
    rest = wt - hi.astype(F32)
    mid = rest.astype(BF16)
    low = (rest - mid.astype(F32)).astype(BF16)
    parts = dot(jnp.concatenate([hi, mid, low], axis=0), lagged_ref[...], 1, 0)
    fitted = parts[:SENSORS] + (parts[SENSORS : 2 * SENSORS] + parts[2 * SENSORS :])
    resid_ref[...] = x_ref[...].astype(F32) - fitted


def on_device(signal, lag_table, window_end):
    blks, grps = lax.axis_size("blk"), lax.axis_size("grp")
    blk, grp = lax.axis_index("blk"), lax.axis_index("grp")
    x = signal[0]
    order = lambda b, g: b * grps + g
    following = [
        (order(b, g), order(b + 1, g) if b + 1 < blks else order(0, g + 1))
        for b in range(blks)
        for g in range(grps)
        if b + 1 < blks or g + 1 < grps
    ]
    tail = lax.ppermute(x[:, ROWS - TILE :], ("blk", "grp"), following)
    lagged, packed = pl.pallas_call(
        gram_kernel,
        out_shape=[
            jax.ShapeDtypeStruct((COLS, ROWS), BF16),
            jax.ShapeDtypeStruct((PACKED, TILE), F32),
        ],
        in_specs=[SMEM, VMEM, VMEM, VMEM],
        out_specs=[VMEM, VMEM],
        compiler_params=pltpu.CompilerParams(vmem_limit_bytes=40 << 20),
    )(window_end, lag_table[None, :], tail, x)

    core, low, high = 2, 4, blks // 8
    at = lambda h, l, c: (h * low + l) * core + c
    near = [[at(h, l, c) for l in range(low)] for h in range(high) for c in range(core)]
    far = [[at(h, l, c) for h in range(high)] for l in range(low) for c in range(core)]
    other = [(i, i ^ 1) for i in range(blks)]
    c_index = blk % 2

    def swap(part, groups):
        return lax.all_to_all(part, "blk", 0, 0, axis_index_groups=groups)

    share = PACKED // blks
    parts = packed.reshape(core, low, high, share, TILE)
    mine = lax.dynamic_index_in_dim(parts, c_index, 0, keepdims=False)
    theirs = lax.dynamic_index_in_dim(parts, 1 - c_index, 0, keepdims=False)
    mine = mine + lax.ppermute(theirs, "blk", other)
    mine = swap(mine, near).sum(0)
    mine = swap(mine, far).sum(0)
    groups = lax.all_to_all(jnp.broadcast_to(mine[None], (grps, share, TILE)), "grp", 0, 0)
    until = (jnp.arange(grps) <= grp)[:, None, None]
    mine = jnp.where(until, groups, 0.0).sum(0)
    mine = swap(jnp.broadcast_to(mine[None], (high, share, TILE)), far)
    mine = swap(jnp.broadcast_to(mine[None], (low, high, share, TILE)), near)
    theirs = lax.ppermute(mine, "blk", other)
    first = jnp.where(c_index == 0, mine, theirs)
    second = jnp.where(c_index == 0, theirs, mine)
    prefix = jnp.stack([first, second]).reshape(PACKED, TILE)

    out_rows = COLS // blks
    factor, coef, resid = pl.pallas_call(
        fit_kernel,
        out_shape=[
            jax.ShapeDtypeStruct((out_rows, COLS), F32),
            jax.ShapeDtypeStruct((out_rows, SENSORS), F32),
            jax.ShapeDtypeStruct((SENSORS, ROWS), F32),
        ],
        in_specs=[SMEM, VMEM, VMEM, VMEM],
        out_specs=[VMEM, VMEM, VMEM],
        scratch_shapes=[
            pltpu.VMEM((COLS, COLS), F32),
            pltpu.VMEM((COLS, TILE), F32),
            pltpu.VMEM((COLS, SENSORS), F32),
        ],
        compiler_params=pltpu.CompilerParams(vmem_limit_bytes=40 << 20),
    )(blk.reshape(1, 1), prefix, lagged, x)
    return factor[None], coef[None], resid[None]


def solution(mesh):
    return jax.shard_map(
        on_device,
        mesh=mesh,
        in_specs=(P("grp", None, "blk"), P(), P("grp", "blk")),
        out_specs=(P("grp", "blk", None), P("grp", "blk", None), P("grp", None, "blk")),
        check_vma=False,
    )
```

```python
import jax
import jax.numpy as jnp
from jax import lax
from jax.experimental import pallas as pl
from jax.experimental.pallas import tpu as pltpu
from jax.sharding import PartitionSpec as P

F32 = jnp.float32
BF16 = jnp.bfloat16
RIDGE = 4.0
SENSORS = 64
LAGS = 8
COLS = 512
ROWS = 512
TILE = 128
NT = COLS // TILE
TILES = [(k, j) for k in range(NT) for j in range(k, NT)]
PACKED = (len(TILES) + NT // 2) * TILE
VMEM = pl.BlockSpec(memory_space=pltpu.VMEM)
SMEM = pl.BlockSpec(memory_space=pltpu.SMEM)


def dot(a, b, ca, cb, precision=None):
    return lax.dot_general(
        a, b, (((ca,), (cb,)), ((), ())), precision=precision, preferred_element_type=F32
    )


def gram_kernel(end_ref, table_ref, tail_ref, x_ref, lagged_ref, packed_ref):
    x = x_ref[...]
    ext = jnp.concatenate([tail_ref[...], x], axis=1).astype(F32)
    pieces = [pltpu.roll(ext, d, 1)[:, TILE:].astype(BF16) for d in range(1, LAGS + 1)]
    canonical = jnp.concatenate(pieces, axis=0)
    pair = lax.broadcasted_iota(jnp.int32, (COLS, COLS), 0)
    chosen = jnp.where(pair == table_ref[...], 1.0, 0.0).astype(BF16)
    lagged = dot(chosen, canonical, 0, 0).astype(BF16)
    lagged_ref[...] = lagged
    time = lax.broadcasted_iota(jnp.int32, (COLS, ROWS), 1)
    masked = jnp.where(time < end_ref[0, 0], lagged.astype(F32), 0.0).astype(BF16)
    eye = (
        lax.broadcasted_iota(jnp.int32, (TILE, TILE), 0)
        == lax.broadcasted_iota(jnp.int32, (TILE, TILE), 1)
    )
    ridge = jnp.where(eye, RIDGE, 0.0)
    n = 0
    for k in range(NT):
        rows = masked[k * TILE : (k + 1) * TILE]
        block = dot(rows, lagged[k * TILE :], 1, 1)
        for j in range(k, NT):
            tile = block[:, (j - k) * TILE : (j - k + 1) * TILE]
            packed_ref[n * TILE : (n + 1) * TILE, :] = tile + ridge if j == k else tile
            n += 1
    cross = dot(masked, x, 1, 1)
    half = COLS // 2
    packed_ref[n * TILE :, :] = jnp.concatenate([cross[:half], cross[half:]], axis=1)


def factor_tile(d_rows):
    n = len(d_rows)
    lane = lax.broadcasted_iota(jnp.int32, (8, TILE), 1)
    sub = lax.broadcasted_iota(jnp.int32, (8, TILE), 0)
    d = list(d_rows)
    x = [jnp.where(lane == 8 * q + sub, 1.0, 0.0) for q in range(n)]

    def col(v, c):
        return jnp.broadcast_to(v[:, c : c + 1], (8, TILE))

    def row(v, i):
        return jnp.broadcast_to(v[i : i + 1, :], (8, TILE))

    for p in range(n):
        base = 8 * p
        c = [col(d[p], base + j) for j in range(8)]
        s = {(i, j): row(c[j], i) for j in range(8) for i in range(j + 1)}
        r = [row(d[p], i) for i in range(8)]
        xr = [row(x[p], i) for i in range(8)]
        cn = [col(d[p + 1], base + j) for j in range(8)] if p + 1 < n else []
        u = {}
        inv = []
        for k in range(8):
            w = lax.rsqrt(s[k, k])
            inv.append(w)
            for j in range(k + 1, 8):
                u[k, j] = s[k, j] * w
            for i in range(k + 1, 8):
                for j in range(i, 8):
                    s[i, j] = s[i, j] - u[k, i] * u[k, j]
            r[k] = r[k] * w
            xr[k] = xr[k] * w
            if cn:
                cn[k] = cn[k] * w
            for i in range(k + 1, 8):
                r[i] = r[i] - u[k, i] * r[k]
                xr[i] = xr[i] - u[k, i] * xr[k]
                if cn:
                    cn[i] = cn[i] - u[k, i] * cn[k]
        if p + 1 < n:
            t = [cn[i] * r[i] for i in range(8)]
            d[p + 1] = d[p + 1] - (((t[0] + t[1]) + (t[2] + t[3])) + ((t[4] + t[5]) + (t[6] + t[7])))
            t = [cn[i] * xr[i] for i in range(8)]
            x[p + 1] = x[p + 1] - (((t[0] + t[1]) + (t[2] + t[3])) + ((t[4] + t[5]) + (t[6] + t[7])))
        if p + 2 < n:
            z = list(r)
            xz = list(xr)
            for k in reversed(range(8)):
                z[k] = z[k] * inv[k]
                xz[k] = xz[k] * inv[k]
                for i in range(k):
                    z[i] = z[i] - u[i, k] * z[k]
                    xz[i] = xz[i] - u[i, k] * xz[k]
            for q in range(p + 2, n):
                cq = [col(d[q], base + j) for j in range(8)]
                t = [cq[i] * z[i] for i in range(8)]
                d[q] = d[q] - (((t[0] + t[1]) + (t[2] + t[3])) + ((t[4] + t[5]) + (t[6] + t[7])))
                t = [cq[i] * xz[i] for i in range(8)]
                x[q] = x[q] - (((t[0] + t[1]) + (t[2] + t[3])) + ((t[4] + t[5]) + (t[6] + t[7])))
        du, dx = r[0], xr[0]
        for i in range(1, 8):
            du = jnp.where(sub == i, r[i], du)
            dx = jnp.where(sub == i, xr[i], dx)
        d[p] = jnp.where(lane >= base + sub, du, 0.0)
        x[p] = dx
    return d, x


def fit_kernel(blk_ref, packed_ref, lagged_ref, x_ref, factor_ref, coef_ref, resid_ref, u_ref, i_ref, w_ref):
    high = lax.Precision.HIGHEST
    half = COLS // 2
    tiles = {}
    for n, (k, j) in enumerate(TILES):
        tiles[k, j] = (n * TILE,)
    base = len(TILES) * TILE
    g = {kj: packed_ref[at : at + TILE, :] for kj, (at,) in tiles.items()}
    b = []
    for k in range(NT):
        at = base + (k * TILE) % half
        lo = (k * TILE // half) * SENSORS
        b.append(packed_ref[at : at + TILE, lo : lo + SENSORS])
    u_ref[...] = jnp.zeros_like(u_ref)
    y = []
    for k in range(NT):
        d, xi = factor_tile([g[k, k][8 * q : 8 * q + 8] for q in range(TILE // 8)])
        ukk = jnp.concatenate(d, axis=0)
        xkk = jnp.concatenate(xi, axis=0)
        i_ref[k * TILE : (k + 1) * TILE, :] = xkk
        u_ref[k * TILE : (k + 1) * TILE, k * TILE : (k + 1) * TILE] = ukk
        panel = {}
        for j in range(k + 1, NT):
            panel[j] = dot(xkk, g[k, j], 1, 0, high)
            u_ref[k * TILE : (k + 1) * TILE, j * TILE : (j + 1) * TILE] = panel[j]
        y.append(dot(xkk, b[k], 1, 0, high))
        for i in range(k + 1, NT):
            for j in range(i, NT):
                g[i, j] = g[i, j] - dot(panel[i], panel[j], 0, 0, high)
            b[i] = b[i] - dot(panel[i], y[k], 0, 0, high)
    w = [None] * NT
    for k in reversed(range(NT)):
        acc = y[k]
        for j in range(k + 1, NT):
            ukj = u_ref[k * TILE : (k + 1) * TILE, j * TILE : (j + 1) * TILE]
            acc = acc - dot(ukj, w[j], 1, 0, high)
        w[k] = dot(i_ref[k * TILE : (k + 1) * TILE, :], acc, 0, 0, high)
        w_ref[k * TILE : (k + 1) * TILE, :] = w[k]
    share = factor_ref.shape[0]
    first = pl.multiple_of(blk_ref[0, 0] * share, 8)
    factor_ref[...] = u_ref[pl.ds(first, share), :] * (1.0 / 128.0)
    coef_ref[...] = w_ref[pl.ds(first, share), :]
    wt = jnp.concatenate([w_ref[...], jnp.zeros((COLS, TILE - SENSORS), F32)], axis=1).T[:SENSORS]
    hi = wt.astype(BF16)
    rest = wt - hi.astype(F32)
    mid = rest.astype(BF16)
    low = (rest - mid.astype(F32)).astype(BF16)
    parts = dot(jnp.concatenate([hi, mid, low], axis=0), lagged_ref[...], 1, 0)
    fitted = parts[:SENSORS] + (parts[SENSORS : 2 * SENSORS] + parts[2 * SENSORS :])
    resid_ref[...] = x_ref[...].astype(F32) - fitted


def on_device(signal, lag_table, window_end):
    blks, grps = lax.axis_size("blk"), lax.axis_size("grp")
    blk, grp = lax.axis_index("blk"), lax.axis_index("grp")
    x = signal[0]
    order = lambda b, g: b * grps + g
    following = [
        (order(b, g), order(b + 1, g) if b + 1 < blks else order(0, g + 1))
        for b in range(blks)
        for g in range(grps)
        if b + 1 < blks or g + 1 < grps
    ]
    tail = lax.ppermute(x[:, ROWS - TILE :], ("blk", "grp"), following)
    lagged, packed = pl.pallas_call(
        gram_kernel,
        out_shape=[
            jax.ShapeDtypeStruct((COLS, ROWS), BF16),
            jax.ShapeDtypeStruct((PACKED, TILE), F32),
        ],
        in_specs=[SMEM, VMEM, VMEM, VMEM],
        out_specs=[VMEM, VMEM],
        compiler_params=pltpu.CompilerParams(vmem_limit_bytes=40 << 20),
    )(window_end, lag_table[None, :], tail, x)

    core, chips = 2, blks // 2
    column = [[z * core + c for z in range(chips)] for c in range(core)]
    other = [(i, i ^ 1) for i in range(blks)]
    c_index = blk % core

    def swap(part):
        return lax.all_to_all(part, "blk", 0, 0, axis_index_groups=column)

    share = PACKED // blks
    parts = packed.reshape(core, chips, share, TILE)
    mine = lax.dynamic_index_in_dim(parts, c_index, 0, keepdims=False)
    theirs = lax.dynamic_index_in_dim(parts, 1 - c_index, 0, keepdims=False)
    mine = mine + lax.ppermute(theirs, "blk", other)
    mine = swap(mine).sum(0)
    groups = lax.all_to_all(jnp.broadcast_to(mine[None], (grps, share, TILE)), "grp", 0, 0)
    until = (jnp.arange(grps) <= grp)[:, None, None]
    mine = jnp.where(until, groups, 0.0).sum(0)
    mine = swap(jnp.broadcast_to(mine[None], (chips, share, TILE)))
    theirs = lax.ppermute(mine, "blk", other)
    first = jnp.where(c_index == 0, mine, theirs)
    second = jnp.where(c_index == 0, theirs, mine)
    prefix = jnp.stack([first, second]).reshape(PACKED, TILE)

    out_rows = COLS // blks
    factor, coef, resid = pl.pallas_call(
        fit_kernel,
        out_shape=[
            jax.ShapeDtypeStruct((out_rows, COLS), F32),
            jax.ShapeDtypeStruct((out_rows, SENSORS), F32),
            jax.ShapeDtypeStruct((SENSORS, ROWS), F32),
        ],
        in_specs=[SMEM, VMEM, VMEM, VMEM],
        out_specs=[VMEM, VMEM, VMEM],
        scratch_shapes=[
            pltpu.VMEM((COLS, COLS), F32),
            pltpu.VMEM((COLS, TILE), F32),
            pltpu.VMEM((COLS, SENSORS), F32),
        ],
        compiler_params=pltpu.CompilerParams(vmem_limit_bytes=40 << 20),
    )(blk.reshape(1, 1), prefix, lagged, x)
    return factor[None], coef[None], resid[None]


def solution(mesh):
    return jax.shard_map(
        on_device,
        mesh=mesh,
        in_specs=(P("grp", None, "blk"), P(), P("grp", "blk")),
        out_specs=(P("grp", "blk", None), P("grp", "blk", None), P("grp", None, "blk")),
        check_vma=False,
    )
```

```python
import jax
import jax.numpy as jnp
from jax import lax
from jax.experimental import pallas as pl
from jax.experimental.pallas import tpu as pltpu
from jax.sharding import PartitionSpec as P

F32 = jnp.float32
BF16 = jnp.bfloat16
RIDGE = 4.0
SENSORS = 64
LAGS = 8
COLS = 512
ROWS = 512
TILE = 128
NT = COLS // TILE
TILES = [(k, j) for k in range(NT) for j in range(k, NT)]
PACKED = (len(TILES) + NT // 2) * TILE
VMEM = pl.BlockSpec(memory_space=pltpu.VMEM)
SMEM = pl.BlockSpec(memory_space=pltpu.SMEM)


def dot(a, b, ca, cb, precision=None):
    return lax.dot_general(
        a, b, (((ca,), (cb,)), ((), ())), precision=precision, preferred_element_type=F32
    )


def gram_kernel(end_ref, table_ref, tail_ref, x_ref, lagged_ref, packed_ref):
    x = x_ref[...]
    ext = jnp.concatenate([tail_ref[...], x], axis=1).astype(F32)
    pieces = [pltpu.roll(ext, d, 1)[:, TILE:].astype(BF16) for d in range(1, LAGS + 1)]
    canonical = jnp.concatenate(pieces, axis=0)
    pair = lax.broadcasted_iota(jnp.int32, (COLS, COLS), 0)
    chosen = jnp.where(pair == table_ref[...], 1.0, 0.0).astype(BF16)
    lagged = dot(chosen, canonical, 0, 0).astype(BF16)
    lagged_ref[...] = lagged
    time = lax.broadcasted_iota(jnp.int32, (COLS, ROWS), 1)
    masked = jnp.where(time < end_ref[0, 0], lagged.astype(F32), 0.0).astype(BF16)
    eye = (
        lax.broadcasted_iota(jnp.int32, (TILE, TILE), 0)
        == lax.broadcasted_iota(jnp.int32, (TILE, TILE), 1)
    )
    ridge = jnp.where(eye, RIDGE, 0.0)
    n = 0
    for k in range(NT):
        rows = masked[k * TILE : (k + 1) * TILE]
        block = dot(rows, lagged[k * TILE :], 1, 1)
        for j in range(k, NT):
            tile = block[:, (j - k) * TILE : (j - k + 1) * TILE]
            packed_ref[n * TILE : (n + 1) * TILE, :] = tile + ridge if j == k else tile
            n += 1
    cross = dot(masked, x, 1, 1)
    half = COLS // 2
    packed_ref[n * TILE :, :] = jnp.concatenate([cross[:half], cross[half:]], axis=1)


def factor_tile(d_rows, rows_ref):
    n = len(d_rows)
    lane = lax.broadcasted_iota(jnp.int32, (8, TILE), 1)
    sub = lax.broadcasted_iota(jnp.int32, (8, TILE), 0)
    d = list(d_rows)
    x = [jnp.where(lane == 8 * q + sub, 1.0, 0.0) for q in range(n)]

    def col(v, c):
        return jnp.broadcast_to(v[:, c : c + 1], (8, TILE))

    def less(v, a, b):
        t = [a[i] * b[i] for i in range(8)]
        return v - (((t[0] + t[1]) + (t[2] + t[3])) + ((t[4] + t[5]) + (t[6] + t[7])))

    for p in range(n):
        base = 8 * p

        def rows_of(v, slot, count):
            at = 8 * (slot + 10 * (p % 2))
            rows_ref[at : at + 8, :] = v
            return [jnp.broadcast_to(rows_ref[at + i : at + i + 1, :], (8, TILE)) for i in range(count)]

        s = {}
        for j in range(8):
            for i, v in enumerate(rows_of(col(d[p], base + j), j, j + 1)):
                s[i, j] = v
        r = rows_of(d[p], 8, 8)
        xr = rows_of(x[p], 9, 8)
        cn = [col(d[p + 1], base + j) for j in range(8)] if p + 1 < n else []
        sets = [v for v in (r, xr, cn) if v]
        u, inv = {}, [None] * 8
        for k in range(0, 8, 2):
            one, off, two = s[k, k], s[k, k + 1], s[k + 1, k + 1]
            w0 = lax.rsqrt(one)
            w1 = lax.rsqrt((one * two - off * off) * one) * one
            inv[k], inv[k + 1] = w0, w1
            u[k, k + 1] = off * w0
            for j in range(k + 2, 8):
                u[k, j] = s[k, j] * w0
                u[k + 1, j] = (s[k + 1, j] - u[k, k + 1] * u[k, j]) * w1
            for i in range(k + 2, 8):
                for j in range(i, 8):
                    s[i, j] = (s[i, j] - u[k, i] * u[k, j]) - u[k + 1, i] * u[k + 1, j]
            for v in sets:
                v[k] = v[k] * w0
                v[k + 1] = (v[k + 1] - u[k, k + 1] * v[k]) * w1
                for i in range(k + 2, 8):
                    v[i] = (v[i] - u[k, i] * v[k]) - u[k + 1, i] * v[k + 1]
        if p + 1 < n:
            d[p + 1] = less(d[p + 1], cn, r)
            x[p + 1] = less(x[p + 1], cn, xr)
        if p + 2 < n:
            z, xz = list(r), list(xr)
            for k in reversed(range(8)):
                for v in (z, xz):
                    v[k] = v[k] * inv[k]
                    for i in range(k):
                        v[i] = v[i] - u[i, k] * v[k]
            for q in range(p + 2, n):
                cq = [col(d[q], base + j) for j in range(8)]
                d[q] = less(d[q], cq, z)
                x[q] = less(x[q], cq, xz)
        du, dx = r[0], xr[0]
        for i in range(1, 8):
            du = jnp.where(sub == i, r[i], du)
            dx = jnp.where(sub == i, xr[i], dx)
        d[p] = jnp.where(lane >= base + sub, du, 0.0)
        x[p] = dx
    return d, x


def fit_kernel(blk_ref, packed_ref, lagged_ref, x_ref, factor_ref, coef_ref, resid_ref, u_ref, w_ref, rows_ref):
    high = lax.Precision.HIGHEST
    half = COLS // 2
    tiles = {}
    for n, (k, j) in enumerate(TILES):
        tiles[k, j] = (n * TILE,)
    base = len(TILES) * TILE
    g = {kj: packed_ref[at : at + TILE, :] for kj, (at,) in tiles.items()}
    b = []
    for k in range(NT):
        at = base + (k * TILE) % half
        lo = (k * TILE // half) * SENSORS
        b.append(packed_ref[at : at + TILE, lo : lo + SENSORS])
    u_ref[...] = jnp.zeros_like(u_ref)
    y = []
    e = {}
    for k in range(NT):
        d, xi = factor_tile([g[k, k][8 * q : 8 * q + 8] for q in range(TILE // 8)], rows_ref)
        ukk = jnp.concatenate(d, axis=0)
        xkk = jnp.concatenate(xi, axis=0)
        u_ref[k * TILE : (k + 1) * TILE, k * TILE : (k + 1) * TILE] = ukk
        panel = {}
        for j in range(k + 1, NT):
            panel[j] = dot(xkk, g[k, j], 1, 0, high)
            u_ref[k * TILE : (k + 1) * TILE, j * TILE : (j + 1) * TILE] = panel[j]
        y.append(dot(xkk, b[k], 1, 0, high))
        e[k, k] = xkk
        for i in range(k):
            e[k, i] = dot(xkk, e[k, i], 1, 0, high)
        for i in range(k + 1, NT):
            for j in range(i, NT):
                g[i, j] = g[i, j] - dot(panel[i], panel[j], 0, 0, high)
            b[i] = b[i] - dot(panel[i], y[k], 0, 0, high)
            for h in range(k + 1):
                past = dot(panel[i], e[k, h], 0, 0, high)
                e[i, h] = e[i, h] - past if (i, h) in e else -past
    for k in range(NT):
        acc = dot(e[k, k], y[k], 0, 0, high)
        for j in range(k + 1, NT):
            acc = acc + dot(e[j, k], y[j], 0, 0, high)
        w_ref[k * TILE : (k + 1) * TILE, :] = acc
    share = factor_ref.shape[0]
    first = pl.multiple_of(blk_ref[0, 0] * share, 8)
    factor_ref[...] = u_ref[pl.ds(first, share), :] * (1.0 / 128.0)
    coef_ref[...] = w_ref[pl.ds(first, share), :]
    wt = jnp.concatenate([w_ref[...], jnp.zeros((COLS, TILE - SENSORS), F32)], axis=1).T[:SENSORS]
    hi = wt.astype(BF16)
    rest = wt - hi.astype(F32)
    mid = rest.astype(BF16)
    low = (rest - mid.astype(F32)).astype(BF16)
    parts = dot(jnp.concatenate([hi, mid, low], axis=0), lagged_ref[...], 1, 0)
    fitted = parts[:SENSORS] + (parts[SENSORS : 2 * SENSORS] + parts[2 * SENSORS :])
    resid_ref[...] = x_ref[...].astype(F32) - fitted


def on_device(signal, lag_table, window_end):
    blks, grps = lax.axis_size("blk"), lax.axis_size("grp")
    blk, grp = lax.axis_index("blk"), lax.axis_index("grp")
    x = signal[0]
    order = lambda b, g: b * grps + g
    following = [
        (order(b, g), order(b + 1, g) if b + 1 < blks else order(0, g + 1))
        for b in range(blks)
        for g in range(grps)
        if b + 1 < blks or g + 1 < grps
    ]
    tail = lax.ppermute(x[:, ROWS - TILE :], ("blk", "grp"), following)
    lagged, packed = pl.pallas_call(
        gram_kernel,
        out_shape=[
            jax.ShapeDtypeStruct((COLS, ROWS), BF16),
            jax.ShapeDtypeStruct((PACKED, TILE), F32),
        ],
        in_specs=[SMEM, VMEM, VMEM, VMEM],
        out_specs=[VMEM, VMEM],
        compiler_params=pltpu.CompilerParams(vmem_limit_bytes=40 << 20),
    )(window_end, lag_table[None, :], tail, x)

    core, chips = 2, blks // 2
    column = [[z * core + c for z in range(chips)] for c in range(core)]
    other = [(i, i ^ 1) for i in range(blks)]
    c_index = blk % core

    def swap(part):
        return lax.all_to_all(part, "blk", 0, 0, axis_index_groups=column)

    share = PACKED // blks
    parts = packed.reshape(core, chips, share, TILE)
    mine = lax.dynamic_index_in_dim(parts, c_index, 0, keepdims=False)
    theirs = lax.dynamic_index_in_dim(parts, 1 - c_index, 0, keepdims=False)
    mine = mine + lax.ppermute(theirs, "blk", other)
    mine = swap(mine).sum(0)
    groups = lax.all_to_all(jnp.broadcast_to(mine[None], (grps, share, TILE)), "grp", 0, 0)
    until = (jnp.arange(grps) <= grp)[:, None, None]
    mine = jnp.where(until, groups, 0.0).sum(0)
    mine = swap(jnp.broadcast_to(mine[None], (chips, share, TILE)))
    theirs = lax.ppermute(mine, "blk", other)
    first = jnp.where(c_index == 0, mine, theirs)
    second = jnp.where(c_index == 0, theirs, mine)
    prefix = jnp.stack([first, second]).reshape(PACKED, TILE)

    out_rows = COLS // blks
    factor, coef, resid = pl.pallas_call(
        fit_kernel,
        out_shape=[
            jax.ShapeDtypeStruct((out_rows, COLS), F32),
            jax.ShapeDtypeStruct((out_rows, SENSORS), F32),
            jax.ShapeDtypeStruct((SENSORS, ROWS), F32),
        ],
        in_specs=[SMEM, VMEM, VMEM, VMEM],
        out_specs=[VMEM, VMEM, VMEM],
        scratch_shapes=[
            pltpu.VMEM((COLS, COLS), F32),
            pltpu.VMEM((COLS, SENSORS), F32),
            pltpu.VMEM((160, TILE), F32),
        ],
        compiler_params=pltpu.CompilerParams(vmem_limit_bytes=40 << 20),
    )(blk.reshape(1, 1), prefix, lagged, x)
    return factor[None], coef[None], resid[None]


def solution(mesh):
    return jax.shard_map(
        on_device,
        mesh=mesh,
        in_specs=(P("grp", None, "blk"), P(), P("grp", "blk")),
        out_specs=(P("grp", "blk", None), P("grp", "blk", None), P("grp", None, "blk")),
        check_vma=False,
    )
```

```python
import jax
import jax.numpy as jnp
from jax import lax
from jax.experimental import pallas as pl
from jax.experimental.pallas import tpu as pltpu
from jax.sharding import PartitionSpec as P

F32 = jnp.float32
BF16 = jnp.bfloat16
RIDGE = 4.0
SENSORS = 64
LAGS = 8
COLS = 512
ROWS = 512
TILE = 128
NT = COLS // TILE
TILES = [(k, j) for k in range(NT) for j in range(k, NT)]
PACKED = (len(TILES) + NT // 2) * TILE
VMEM = pl.BlockSpec(memory_space=pltpu.VMEM)
SMEM = pl.BlockSpec(memory_space=pltpu.SMEM)


def dot(a, b, ca, cb, precision=None):
    return lax.dot_general(
        a, b, (((ca,), (cb,)), ((), ())), precision=precision, preferred_element_type=F32
    )


def gram_kernel(end_ref, table_ref, tail_ref, x_ref, lagged_ref, packed_ref):
    x = x_ref[...]
    ext = jnp.concatenate([tail_ref[...], x], axis=1).astype(F32)
    pieces = [pltpu.roll(ext, d, 1)[:, TILE:].astype(BF16) for d in range(1, LAGS + 1)]
    canonical = jnp.concatenate(pieces, axis=0)
    pair = lax.broadcasted_iota(jnp.int32, (COLS, COLS), 0)
    chosen = jnp.where(pair == table_ref[...], 1.0, 0.0).astype(BF16)
    lagged = dot(chosen, canonical, 0, 0).astype(BF16)
    lagged_ref[...] = lagged
    time = lax.broadcasted_iota(jnp.int32, (COLS, ROWS), 1)
    masked = jnp.where(time < end_ref[0, 0], lagged.astype(F32), 0.0).astype(BF16)
    eye = (
        lax.broadcasted_iota(jnp.int32, (TILE, TILE), 0)
        == lax.broadcasted_iota(jnp.int32, (TILE, TILE), 1)
    )
    ridge = jnp.where(eye, RIDGE, 0.0)
    n = 0
    for k in range(NT):
        rows = masked[k * TILE : (k + 1) * TILE]
        block = dot(rows, lagged[k * TILE :], 1, 1)
        for j in range(k, NT):
            tile = block[:, (j - k) * TILE : (j - k + 1) * TILE]
            packed_ref[n * TILE : (n + 1) * TILE, :] = tile + ridge if j == k else tile
            n += 1
    cross = dot(masked, x, 1, 1)
    half = COLS // 2
    packed_ref[n * TILE :, :] = jnp.concatenate([cross[:half], cross[half:]], axis=1)


def factor_tile(d_rows, rows_ref):
    n = len(d_rows)
    lane = lax.broadcasted_iota(jnp.int32, (8, TILE), 1)
    sub = lax.broadcasted_iota(jnp.int32, (8, TILE), 0)
    d = list(d_rows)
    x = [jnp.where(lane == 8 * q + sub, 1.0, 0.0) for q in range(n)]

    def col(v, c):
        return jnp.broadcast_to(v[:, c : c + 1], (8, TILE))

    def less(v, a, b):
        t = [a[i] * b[i] for i in range(8)]
        return v - (((t[0] + t[1]) + (t[2] + t[3])) + ((t[4] + t[5]) + (t[6] + t[7])))

    for p in range(n):
        base = 8 * p

        def rows_of(v, slot, count):
            at = 8 * (slot + 10 * (p % 2))
            rows_ref[at : at + 8, :] = v
            return [jnp.broadcast_to(rows_ref[at + i : at + i + 1, :], (8, TILE)) for i in range(count)]

        s = {}
        for j in range(8):
            for i, v in enumerate(rows_of(col(d[p], base + j), j, j + 1)):
                s[i, j] = v
        r = rows_of(d[p], 8, 8)
        xr = rows_of(x[p], 9, 8)
        cn = [col(d[p + 1], base + j) for j in range(8)] if p + 1 < n else []
        sets = [v for v in (r, xr, cn) if v]
        u, inv = {}, [None] * 8
        for k in range(0, 8, 2):
            one, off, two = s[k, k], s[k, k + 1], s[k + 1, k + 1]
            w0 = lax.rsqrt(one)
            w1 = lax.rsqrt((one * two - off * off) * one) * one
            inv[k], inv[k + 1] = w0, w1
            u[k, k + 1] = off * w0
            for j in range(k + 2, 8):
                u[k, j] = s[k, j] * w0
                u[k + 1, j] = (s[k + 1, j] - u[k, k + 1] * u[k, j]) * w1
            for i in range(k + 2, 8):
                for j in range(i, 8):
                    s[i, j] = (s[i, j] - u[k, i] * u[k, j]) - u[k + 1, i] * u[k + 1, j]
            for v in sets:
                v[k] = v[k] * w0
                v[k + 1] = (v[k + 1] - u[k, k + 1] * v[k]) * w1
                for i in range(k + 2, 8):
                    v[i] = (v[i] - u[k, i] * v[k]) - u[k + 1, i] * v[k + 1]
        if p + 1 < n:
            d[p + 1] = less(d[p + 1], cn, r)
            x[p + 1] = less(x[p + 1], cn, xr)
        if p + 2 < n:
            z, xz = list(r), list(xr)
            for k in reversed(range(8)):
                for v in (z, xz):
                    v[k] = v[k] * inv[k]
                    for i in range(k):
                        v[i] = v[i] - u[i, k] * v[k]
            for q in range(p + 2, n):
                cq = [col(d[q], base + j) for j in range(8)]
                d[q] = less(d[q], cq, z)
                x[q] = less(x[q], cq, xz)
        du, dx = r[0], xr[0]
        for i in range(1, 8):
            du = jnp.where(sub == i, r[i], du)
            dx = jnp.where(sub == i, xr[i], dx)
        d[p] = jnp.where(lane >= base + sub, du, 0.0)
        x[p] = dx
    return d, x


def fit_kernel(blk_ref, packed_ref, lagged_ref, x_ref, factor_ref, coef_ref, resid_ref, u_ref, w_ref, rows_ref):
    high = lax.Precision.HIGHEST
    half = COLS // 2
    tiles = {}
    for n, (k, j) in enumerate(TILES):
        tiles[k, j] = (n * TILE,)
    base = len(TILES) * TILE
    g = {kj: packed_ref[at : at + TILE, :] for kj, (at,) in tiles.items()}
    b = []
    for k in range(NT):
        at = base + (k * TILE) % half
        lo = (k * TILE // half) * SENSORS
        b.append(packed_ref[at : at + TILE, lo : lo + SENSORS])
    u_ref[...] = jnp.zeros_like(u_ref)
    y = []
    e = {}
    for k in range(NT):
        d, xi = factor_tile([g[k, k][8 * q : 8 * q + 8] for q in range(TILE // 8)], rows_ref)
        ukk = jnp.concatenate(d, axis=0)
        xkk = jnp.concatenate(xi, axis=0)
        u_ref[k * TILE : (k + 1) * TILE, k * TILE : (k + 1) * TILE] = ukk
        panel = {}
        for j in range(k + 1, NT):
            panel[j] = dot(xkk, g[k, j], 1, 0, high)
            u_ref[k * TILE : (k + 1) * TILE, j * TILE : (j + 1) * TILE] = panel[j]
        y.append(dot(xkk, b[k], 1, 0, high))
        e[k, k] = xkk
        for i in range(k):
            e[k, i] = dot(xkk, e[k, i], 1, 0, high)
        for i in range(k + 1, NT):
            for j in range(i, NT):
                g[i, j] = g[i, j] - dot(panel[i], panel[j], 0, 0, high)
            b[i] = b[i] - dot(panel[i], y[k], 0, 0, high)
            for h in range(k + 1):
                past = dot(panel[i], e[k, h], 0, 0, high)
                e[i, h] = e[i, h] - past if (i, h) in e else -past
    for k in range(NT):
        acc = dot(e[k, k], y[k], 0, 0, high)
        for j in range(k + 1, NT):
            acc = acc + dot(e[j, k], y[j], 0, 0, high)
        w_ref[k * TILE : (k + 1) * TILE, :] = acc
    share = factor_ref.shape[0]
    first = pl.multiple_of(blk_ref[0, 0] * share, 8)
    factor_ref[...] = u_ref[pl.ds(first, share), :] * (1.0 / 128.0)
    coef_ref[...] = w_ref[pl.ds(first, share), :]
    wt = jnp.concatenate([w_ref[...], jnp.zeros((COLS, TILE - SENSORS), F32)], axis=1).T[:SENSORS]
    hi = wt.astype(BF16)
    rest = wt - hi.astype(F32)
    mid = rest.astype(BF16)
    low = (rest - mid.astype(F32)).astype(BF16)
    parts = dot(jnp.concatenate([hi, mid, low], axis=0), lagged_ref[...], 1, 0)
    fitted = parts[:SENSORS] + (parts[SENSORS : 2 * SENSORS] + parts[2 * SENSORS :])
    resid_ref[...] = x_ref[...].astype(F32) - fitted


def on_device(signal, lag_table, window_end):
    blks, grps = lax.axis_size("blk"), lax.axis_size("grp")
    blk, grp = lax.axis_index("blk"), lax.axis_index("grp")
    x = signal[0]
    order = lambda b, g: b * grps + g
    following = [
        (order(b, g), order(b + 1, g) if b + 1 < blks else order(0, g + 1))
        for b in range(blks)
        for g in range(grps)
        if b + 1 < blks or g + 1 < grps
    ]
    tail = lax.ppermute(x[:, ROWS - TILE :], ("blk", "grp"), following)
    lagged, packed = pl.pallas_call(
        gram_kernel,
        out_shape=[
            jax.ShapeDtypeStruct((COLS, ROWS), BF16),
            jax.ShapeDtypeStruct((PACKED, TILE), F32),
        ],
        in_specs=[SMEM, VMEM, VMEM, VMEM],
        out_specs=[VMEM, VMEM],
        compiler_params=pltpu.CompilerParams(vmem_limit_bytes=40 << 20),
    )(window_end, lag_table[None, :], tail, x)

    core, chips = 2, blks // 2
    column = [[z * core + c for z in range(chips)] for c in range(core)]
    other = [(i, i ^ 1) for i in range(blks)]
    c_index = blk % core

    def swap(part):
        return lax.all_to_all(part, "blk", 0, 0, axis_index_groups=column)

    share = PACKED // blks
    parts = packed.reshape(chips, core, share, TILE)
    mine = lax.dynamic_index_in_dim(parts, c_index, 1, keepdims=False)
    theirs = lax.dynamic_index_in_dim(parts, 1 - c_index, 1, keepdims=False)
    mine = mine + lax.ppermute(theirs, "blk", other)
    mine = swap(mine).sum(0)
    groups = lax.all_to_all(jnp.broadcast_to(mine[None], (grps, share, TILE)), "grp", 0, 0)
    until = (jnp.arange(grps) <= grp)[:, None, None]
    mine = jnp.where(until, groups, 0.0).sum(0)
    prefix = lax.all_gather(mine, "blk", axis=0, tiled=True)

    out_rows = COLS // blks
    factor, coef, resid = pl.pallas_call(
        fit_kernel,
        out_shape=[
            jax.ShapeDtypeStruct((out_rows, COLS), F32),
            jax.ShapeDtypeStruct((out_rows, SENSORS), F32),
            jax.ShapeDtypeStruct((SENSORS, ROWS), F32),
        ],
        in_specs=[SMEM, VMEM, VMEM, VMEM],
        out_specs=[VMEM, VMEM, VMEM],
        scratch_shapes=[
            pltpu.VMEM((COLS, COLS), F32),
            pltpu.VMEM((COLS, SENSORS), F32),
            pltpu.VMEM((160, TILE), F32),
        ],
        compiler_params=pltpu.CompilerParams(vmem_limit_bytes=40 << 20),
    )(blk.reshape(1, 1), prefix, lagged, x)
    return factor[None], coef[None], resid[None]


def solution(mesh):
    return jax.shard_map(
        on_device,
        mesh=mesh,
        in_specs=(P("grp", None, "blk"), P(), P("grp", "blk")),
        out_specs=(P("grp", "blk", None), P("grp", "blk", None), P("grp", None, "blk")),
        check_vma=False,
    )
```

```python
import jax
import jax.numpy as jnp
from jax import lax
from jax.experimental import pallas as pl
from jax.experimental.pallas import tpu as pltpu
from jax.sharding import PartitionSpec as P

F32 = jnp.float32
BF16 = jnp.bfloat16
RIDGE = 4.0
SENSORS = 64
LAGS = 8
COLS = 512
ROWS = 512
TILE = 128
NT = COLS // TILE
TILES = [(k, j) for k in range(NT) for j in range(k + 1, NT)]
PACKED = (len(TILES) + NT // 2 + NT // 2) * TILE
SPARE = 8
VMEM = pl.BlockSpec(memory_space=pltpu.VMEM)
SMEM = pl.BlockSpec(memory_space=pltpu.SMEM)


def dot(a, b, ca, cb, precision=None):
    return lax.dot_general(
        a, b, (((ca,), (cb,)), ((), ())), precision=precision, preferred_element_type=F32
    )


def gram_kernel(end_ref, table_ref, tail_ref, x_ref, lagged_ref, packed_ref, spare_ref):
    x = x_ref[...]
    ext = jnp.concatenate([tail_ref[...], x], axis=1).astype(F32)
    pieces = [pltpu.roll(ext, d, 1)[:, TILE:].astype(BF16) for d in range(1, LAGS + 1)]
    canonical = jnp.concatenate(pieces, axis=0)
    pair = lax.broadcasted_iota(jnp.int32, (COLS, COLS), 0)
    chosen = jnp.where(pair == table_ref[...], 1.0, 0.0).astype(BF16)
    lagged = dot(chosen, canonical, 0, 0).astype(BF16)
    lagged_ref[...] = lagged
    time = lax.broadcasted_iota(jnp.int32, (COLS, ROWS), 1)
    masked = jnp.where(time < end_ref[0, 0], lagged.astype(F32), 0.0).astype(BF16)
    row = lax.broadcasted_iota(jnp.int32, (TILE, TILE), 0)
    column = lax.broadcasted_iota(jnp.int32, (TILE, TILE), 1)
    spare_ref[...] = jnp.zeros_like(spare_ref)
    for k in range(NT):
        rows = masked[k * TILE : (k + 1) * TILE]
        block = dot(rows, lagged[k * TILE :], 1, 1)
        for j in range(k + 1, NT):
            n = TILES.index((k, j)) * TILE
            packed_ref[n : n + TILE, :] = block[:, (j - k) * TILE : (j - k + 1) * TILE]
        tile = block[:, :TILE] + jnp.where(row == column, RIDGE, 0.0)
        if k % 2 == 0:
            first = tile
        else:
            n = (len(TILES) + k // 2) * TILE
            packed_ref[n : n + TILE, :] = jnp.where(row <= column, first, tile)
            spare_ref[k // 2 : k // 2 + 1, :] = jnp.sum(
                jnp.where(row == column, tile, 0.0), axis=0, keepdims=True
            )
    cross = dot(masked, x, 1, 1)
    half = COLS // 2
    n = (len(TILES) + NT // 2) * TILE
    packed_ref[n:, :] = jnp.concatenate([cross[:half], cross[half:]], axis=1)


def factor_tile(d_rows, rows_ref):
    n = len(d_rows)
    lane = lax.broadcasted_iota(jnp.int32, (8, TILE), 1)
    sub = lax.broadcasted_iota(jnp.int32, (8, TILE), 0)
    d = list(d_rows)
    x = [jnp.where(lane == 8 * q + sub, 1.0, 0.0) for q in range(n)]

    def col(v, c):
        return jnp.broadcast_to(v[:, c : c + 1], (8, TILE))

    def less(v, a, b):
        t = [a[i] * b[i] for i in range(8)]
        return v - (((t[0] + t[1]) + (t[2] + t[3])) + ((t[4] + t[5]) + (t[6] + t[7])))

    for p in range(n):
        base = 8 * p

        def rows_of(v, slot, count):
            at = 8 * (slot + 10 * (p % 2))
            rows_ref[at : at + 8, :] = v
            return [jnp.broadcast_to(rows_ref[at + i : at + i + 1, :], (8, TILE)) for i in range(count)]

        s = {}
        for j in range(8):
            for i, v in enumerate(rows_of(col(d[p], base + j), j, j + 1)):
                s[i, j] = v
        r = rows_of(d[p], 8, 8)
        xr = rows_of(x[p], 9, 8)
        cn = [col(d[p + 1], base + j) for j in range(8)] if p + 1 < n else []
        sets = [v for v in (r, xr, cn) if v]
        u, inv = {}, [None] * 8
        for k in range(0, 8, 2):
            one, off, two = s[k, k], s[k, k + 1], s[k + 1, k + 1]
            w0 = lax.rsqrt(one)
            w1 = lax.rsqrt((one * two - off * off) * one) * one
            inv[k], inv[k + 1] = w0, w1
            u[k, k + 1] = off * w0
            for j in range(k + 2, 8):
                u[k, j] = s[k, j] * w0
                u[k + 1, j] = (s[k + 1, j] - u[k, k + 1] * u[k, j]) * w1
            for i in range(k + 2, 8):
                for j in range(i, 8):
                    s[i, j] = (s[i, j] - u[k, i] * u[k, j]) - u[k + 1, i] * u[k + 1, j]
            for v in sets:
                v[k] = v[k] * w0
                v[k + 1] = (v[k + 1] - u[k, k + 1] * v[k]) * w1
                for i in range(k + 2, 8):
                    v[i] = (v[i] - u[k, i] * v[k]) - u[k + 1, i] * v[k + 1]
        if p + 1 < n:
            d[p + 1] = less(d[p + 1], cn, r)
            x[p + 1] = less(x[p + 1], cn, xr)
        if p + 2 < n:
            z, xz = list(r), list(xr)
            for k in reversed(range(8)):
                for v in (z, xz):
                    v[k] = v[k] * inv[k]
                    for i in range(k):
                        v[i] = v[i] - u[i, k] * v[k]
            for q in range(p + 2, n):
                cq = [col(d[q], base + j) for j in range(8)]
                d[q] = less(d[q], cq, z)
                x[q] = less(x[q], cq, xz)
        du, dx = r[0], xr[0]
        for i in range(1, 8):
            du = jnp.where(sub == i, r[i], du)
            dx = jnp.where(sub == i, xr[i], dx)
        d[p] = jnp.where(lane >= base + sub, du, 0.0)
        x[p] = dx
    return d, x


def fit_kernel(blk_ref, packed_ref, lagged_ref, x_ref, factor_ref, coef_ref, resid_ref, u_ref, w_ref, rows_ref):
    high = lax.Precision.HIGHEST
    half = COLS // 2
    devices = COLS // factor_ref.shape[0]
    share = PACKED // devices
    pitch = share + SPARE

    def packed_rows(start):
        pieces, at = [], start
        while at < start + TILE:
            stop = min(start + TILE, (at // share + 1) * share)
            lo = (at // share) * pitch + at % share
            pieces.append(packed_ref[lo : lo + stop - at, :])
            at = stop
        return jnp.concatenate(pieces, axis=0)

    spare = packed_ref[share:pitch, :]
    for i in range(1, devices):
        spare = spare + packed_ref[i * pitch + share : (i + 1) * pitch, :]
    row = lax.broadcasted_iota(jnp.int32, (TILE, TILE), 0)
    column = lax.broadcasted_iota(jnp.int32, (TILE, TILE), 1)
    g = {kj: packed_rows(n * TILE) for n, kj in enumerate(TILES)}
    for k in range(0, NT, 2):
        both = packed_rows((len(TILES) + k // 2) * TILE)
        flipped = both.T
        diagonal = jnp.broadcast_to(spare[k // 2 : k // 2 + 1, :], (TILE, TILE))
        g[k, k] = jnp.where(row <= column, both, flipped)
        other = jnp.where(row > column, both, flipped)
        g[k + 1, k + 1] = jnp.where(row == column, diagonal, other)
    base = (len(TILES) + NT // 2) * TILE
    b = []
    for k in range(NT):
        lo = (k * TILE // half) * SENSORS
        b.append(packed_rows(base + (k * TILE) % half)[:, lo : lo + SENSORS])
    u_ref[...] = jnp.zeros_like(u_ref)
    y = []
    e = {}
    for k in range(NT):
        d, xi = factor_tile([g[k, k][8 * q : 8 * q + 8] for q in range(TILE // 8)], rows_ref)
        ukk = jnp.concatenate(d, axis=0)
        xkk = jnp.concatenate(xi, axis=0)
        u_ref[k * TILE : (k + 1) * TILE, k * TILE : (k + 1) * TILE] = ukk
        panel = {}
        for j in range(k + 1, NT):
            panel[j] = dot(xkk, g[k, j], 1, 0, high)
            u_ref[k * TILE : (k + 1) * TILE, j * TILE : (j + 1) * TILE] = panel[j]
        y.append(dot(xkk, b[k], 1, 0, high))
        e[k, k] = xkk
        for i in range(k):
            e[k, i] = dot(xkk, e[k, i], 1, 0, high)
        for i in range(k + 1, NT):
            for j in range(i, NT):
                g[i, j] = g[i, j] - dot(panel[i], panel[j], 0, 0, high)
            b[i] = b[i] - dot(panel[i], y[k], 0, 0, high)
            for h in range(k + 1):
                past = dot(panel[i], e[k, h], 0, 0, high)
                e[i, h] = e[i, h] - past if (i, h) in e else -past
    for k in range(NT):
        acc = dot(e[k, k], y[k], 0, 0, high)
        for j in range(k + 1, NT):
            acc = acc + dot(e[j, k], y[j], 0, 0, high)
        w_ref[k * TILE : (k + 1) * TILE, :] = acc
    share = factor_ref.shape[0]
    first = pl.multiple_of(blk_ref[0, 0] * share, 8)
    factor_ref[...] = u_ref[pl.ds(first, share), :] * (1.0 / 128.0)
    coef_ref[...] = w_ref[pl.ds(first, share), :]
    wt = jnp.concatenate([w_ref[...], jnp.zeros((COLS, TILE - SENSORS), F32)], axis=1).T[:SENSORS]
    hi = wt.astype(BF16)
    rest = wt - hi.astype(F32)
    mid = rest.astype(BF16)
    low = (rest - mid.astype(F32)).astype(BF16)
    parts = dot(jnp.concatenate([hi, mid, low], axis=0), lagged_ref[...], 1, 0)
    fitted = parts[:SENSORS] + (parts[SENSORS : 2 * SENSORS] + parts[2 * SENSORS :])
    resid_ref[...] = x_ref[...].astype(F32) - fitted


def on_device(signal, lag_table, window_end):
    blks, grps = lax.axis_size("blk"), lax.axis_size("grp")
    blk, grp = lax.axis_index("blk"), lax.axis_index("grp")
    x = signal[0]
    order = lambda b, g: b * grps + g
    following = [
        (order(b, g), order(b + 1, g) if b + 1 < blks else order(0, g + 1))
        for b in range(blks)
        for g in range(grps)
        if b + 1 < blks or g + 1 < grps
    ]
    tail = lax.ppermute(x[:, ROWS - TILE :], ("blk", "grp"), following)
    lagged, packed, spare = pl.pallas_call(
        gram_kernel,
        out_shape=[
            jax.ShapeDtypeStruct((COLS, ROWS), BF16),
            jax.ShapeDtypeStruct((PACKED, TILE), F32),
            jax.ShapeDtypeStruct((SPARE, TILE), F32),
        ],
        in_specs=[SMEM, VMEM, VMEM, VMEM],
        out_specs=[VMEM, VMEM, VMEM],
        compiler_params=pltpu.CompilerParams(vmem_limit_bytes=40 << 20),
    )(window_end, lag_table[None, :], tail, x)

    core, chips = 2, blks // 2
    column = [[z * core + c for z in range(chips)] for c in range(core)]
    other = [(i, i ^ 1) for i in range(blks)]
    c_index = blk % core

    def swap(part):
        return lax.all_to_all(part, "blk", 0, 0, axis_index_groups=column)

    share = PACKED // blks
    parts = packed.reshape(chips, core, share, TILE)
    mine = lax.dynamic_index_in_dim(parts, c_index, 1, keepdims=False)
    theirs = lax.dynamic_index_in_dim(parts, 1 - c_index, 1, keepdims=False)
    mine = mine + lax.ppermute(theirs, "blk", other)
    mine = jnp.concatenate([swap(mine).sum(0), spare], axis=0)
    groups = lax.all_to_all(jnp.broadcast_to(mine[None], (grps, *mine.shape)), "grp", 0, 0)
    until = (jnp.arange(grps) <= grp)[:, None, None]
    mine = jnp.where(until, groups, 0.0).sum(0)
    prefix = lax.all_gather(mine, "blk", axis=0, tiled=True)

    out_rows = COLS // blks
    factor, coef, resid = pl.pallas_call(
        fit_kernel,
        out_shape=[
            jax.ShapeDtypeStruct((out_rows, COLS), F32),
            jax.ShapeDtypeStruct((out_rows, SENSORS), F32),
            jax.ShapeDtypeStruct((SENSORS, ROWS), F32),
        ],
        in_specs=[SMEM, VMEM, VMEM, VMEM],
        out_specs=[VMEM, VMEM, VMEM],
        scratch_shapes=[
            pltpu.VMEM((COLS, COLS), F32),
            pltpu.VMEM((COLS, SENSORS), F32),
            pltpu.VMEM((160, TILE), F32),
        ],
        compiler_params=pltpu.CompilerParams(vmem_limit_bytes=40 << 20),
    )(blk.reshape(1, 1), prefix, lagged, x)
    return factor[None], coef[None], resid[None]


def solution(mesh):
    return jax.shard_map(
        on_device,
        mesh=mesh,
        in_specs=(P("grp", None, "blk"), P(), P("grp", "blk")),
        out_specs=(P("grp", "blk", None), P("grp", "blk", None), P("grp", None, "blk")),
        check_vma=False,
    )
```

```python
import jax
import jax.numpy as jnp
from jax import lax
from jax.experimental import pallas as pl
from jax.experimental.pallas import tpu as pltpu
from jax.sharding import PartitionSpec as P

F32 = jnp.float32
BF16 = jnp.bfloat16
RIDGE = 4.0
SENSORS = 64
LAGS = 8
COLS = 512
ROWS = 512
TILE = 128
NT = COLS // TILE
TILES = [(k, j) for k in range(NT) for j in range(k + 1, NT)]
PACKED = (len(TILES) + NT // 2 + NT // 2) * TILE
SPARE = 8
VMEM = pl.BlockSpec(memory_space=pltpu.VMEM)
SMEM = pl.BlockSpec(memory_space=pltpu.SMEM)


def dot(a, b, ca, cb, precision=None):
    return lax.dot_general(
        a, b, (((ca,), (cb,)), ((), ())), precision=precision, preferred_element_type=F32
    )


def gram_kernel(end_ref, grp_ref, table_ref, tail_ref, x_ref, lagged_ref, packed_ref, spare_ref, until_ref):
    x = x_ref[...]
    ext = jnp.concatenate([tail_ref[...], x], axis=1).astype(F32)
    pieces = [pltpu.roll(ext, d, 1)[:, TILE:].astype(BF16) for d in range(1, LAGS + 1)]
    canonical = jnp.concatenate(pieces, axis=0)
    pair = lax.broadcasted_iota(jnp.int32, (COLS, COLS), 0)
    chosen = jnp.where(pair == table_ref[...], 1.0, 0.0).astype(BF16)
    lagged = dot(chosen, canonical, 0, 0).astype(BF16)
    lagged_ref[...] = lagged
    time = lax.broadcasted_iota(jnp.int32, (COLS, ROWS), 1)
    masked = jnp.where(time < end_ref[0, 0], lagged.astype(F32), 0.0).astype(BF16)
    row = lax.broadcasted_iota(jnp.int32, (TILE, TILE), 0)
    column = lax.broadcasted_iota(jnp.int32, (TILE, TILE), 1)
    spare_ref[...] = jnp.zeros_like(spare_ref)
    group = lax.broadcasted_iota(jnp.int32, until_ref.shape, 0)
    until_ref[...] = jnp.where(group <= grp_ref[0, 0], 1.0, 0.0)
    for k in range(NT):
        rows = masked[k * TILE : (k + 1) * TILE]
        block = dot(rows, lagged[k * TILE :], 1, 1)
        for j in range(k + 1, NT):
            n = TILES.index((k, j)) * TILE
            packed_ref[n : n + TILE, :] = block[:, (j - k) * TILE : (j - k + 1) * TILE]
        tile = block[:, :TILE] + jnp.where(row == column, RIDGE, 0.0)
        if k % 2 == 0:
            first = tile
        else:
            n = (len(TILES) + k // 2) * TILE
            packed_ref[n : n + TILE, :] = jnp.where(row <= column, first, tile)
            spare_ref[k // 2 : k // 2 + 1, :] = jnp.sum(
                jnp.where(row == column, tile, 0.0), axis=0, keepdims=True
            )
    cross = dot(masked, x, 1, 1)
    half = COLS // 2
    n = (len(TILES) + NT // 2) * TILE
    packed_ref[n:, :] = jnp.concatenate([cross[:half], cross[half:]], axis=1)


def factor_tile(d_rows, rows_ref):
    n = len(d_rows)
    lane = lax.broadcasted_iota(jnp.int32, (8, TILE), 1)
    sub = lax.broadcasted_iota(jnp.int32, (8, TILE), 0)
    d = list(d_rows)
    x = [jnp.where(lane == 8 * q + sub, 1.0, 0.0) for q in range(n)]

    def col(v, c):
        return jnp.broadcast_to(v[:, c : c + 1], (8, TILE))

    def less(v, a, b):
        t = [a[i] * b[i] for i in range(8)]
        return v - (((t[0] + t[1]) + (t[2] + t[3])) + ((t[4] + t[5]) + (t[6] + t[7])))

    for p in range(n):
        base = 8 * p

        def rows_of(v, slot, count):
            at = 8 * (slot + 10 * (p % 2))
            rows_ref[at : at + 8, :] = v
            return [jnp.broadcast_to(rows_ref[at + i : at + i + 1, :], (8, TILE)) for i in range(count)]

        s = {}
        for j in range(8):
            for i, v in enumerate(rows_of(col(d[p], base + j), j, j + 1)):
                s[i, j] = v
        r = rows_of(d[p], 8, 8)
        xr = rows_of(x[p], 9, 8)
        cn = [col(d[p + 1], base + j) for j in range(8)] if p + 1 < n else []
        sets = [v for v in (r, xr, cn) if v]
        u, inv = {}, [None] * 8
        for k in range(0, 8, 2):
            one, off, two = s[k, k], s[k, k + 1], s[k + 1, k + 1]
            w0 = lax.rsqrt(one)
            w1 = lax.rsqrt((one * two - off * off) * one) * one
            inv[k], inv[k + 1] = w0, w1
            u[k, k + 1] = off * w0
            for j in range(k + 2, 8):
                u[k, j] = s[k, j] * w0
                u[k + 1, j] = (s[k + 1, j] - u[k, k + 1] * u[k, j]) * w1
            for i in range(k + 2, 8):
                for j in range(i, 8):
                    s[i, j] = (s[i, j] - u[k, i] * u[k, j]) - u[k + 1, i] * u[k + 1, j]
            for v in sets:
                v[k] = v[k] * w0
                v[k + 1] = (v[k + 1] - u[k, k + 1] * v[k]) * w1
                for i in range(k + 2, 8):
                    v[i] = (v[i] - u[k, i] * v[k]) - u[k + 1, i] * v[k + 1]
        if p + 1 < n:
            d[p + 1] = less(d[p + 1], cn, r)
            x[p + 1] = less(x[p + 1], cn, xr)
        if p + 2 < n:
            z, xz = list(r), list(xr)
            for k in reversed(range(8)):
                for v in (z, xz):
                    v[k] = v[k] * inv[k]
                    for i in range(k):
                        v[i] = v[i] - u[i, k] * v[k]
            for q in range(p + 2, n):
                cq = [col(d[q], base + j) for j in range(8)]
                d[q] = less(d[q], cq, z)
                x[q] = less(x[q], cq, xz)
        du, dx = r[0], xr[0]
        for i in range(1, 8):
            du = jnp.where(sub == i, r[i], du)
            dx = jnp.where(sub == i, xr[i], dx)
        d[p] = jnp.where(lane >= base + sub, du, 0.0)
        x[p] = dx
    return d, x


def fit_kernel(blk_ref, packed_ref, lagged_ref, x_ref, factor_ref, coef_ref, resid_ref, u_ref, w_ref, rows_ref):
    high = lax.Precision.HIGHEST
    half = COLS // 2
    devices = COLS // factor_ref.shape[0]
    share = PACKED // devices
    pitch = share + SPARE

    def packed_rows(start):
        pieces, at = [], start
        while at < start + TILE:
            stop = min(start + TILE, (at // share + 1) * share)
            lo = (at // share) * pitch + at % share
            pieces.append(packed_ref[lo : lo + stop - at, :])
            at = stop
        return jnp.concatenate(pieces, axis=0)

    spare = packed_ref[share:pitch, :]
    for i in range(1, devices):
        spare = spare + packed_ref[i * pitch + share : (i + 1) * pitch, :]
    row = lax.broadcasted_iota(jnp.int32, (TILE, TILE), 0)
    column = lax.broadcasted_iota(jnp.int32, (TILE, TILE), 1)
    g = {kj: packed_rows(n * TILE) for n, kj in enumerate(TILES)}
    for k in range(0, NT, 2):
        both = packed_rows((len(TILES) + k // 2) * TILE)
        flipped = both.T
        diagonal = jnp.broadcast_to(spare[k // 2 : k // 2 + 1, :], (TILE, TILE))
        g[k, k] = jnp.where(row <= column, both, flipped)
        other = jnp.where(row > column, both, flipped)
        g[k + 1, k + 1] = jnp.where(row == column, diagonal, other)
    base = (len(TILES) + NT // 2) * TILE
    b = []
    for k in range(NT):
        lo = (k * TILE // half) * SENSORS
        b.append(packed_rows(base + (k * TILE) % half)[:, lo : lo + SENSORS])
    u_ref[...] = jnp.zeros_like(u_ref)
    y = []
    e = {}
    for k in range(NT):
        d, xi = factor_tile([g[k, k][8 * q : 8 * q + 8] for q in range(TILE // 8)], rows_ref)
        ukk = jnp.concatenate(d, axis=0)
        xkk = jnp.concatenate(xi, axis=0)
        u_ref[k * TILE : (k + 1) * TILE, k * TILE : (k + 1) * TILE] = ukk
        panel = {}
        for j in range(k + 1, NT):
            panel[j] = dot(xkk, g[k, j], 1, 0, high)
            u_ref[k * TILE : (k + 1) * TILE, j * TILE : (j + 1) * TILE] = panel[j]
        y.append(dot(xkk, b[k], 1, 0, high))
        e[k, k] = xkk
        for i in range(k):
            e[k, i] = dot(xkk, e[k, i], 1, 0, high)
        for i in range(k + 1, NT):
            for j in range(i, NT):
                g[i, j] = g[i, j] - dot(panel[i], panel[j], 0, 0, high)
            b[i] = b[i] - dot(panel[i], y[k], 0, 0, high)
            for h in range(k + 1):
                past = dot(panel[i], e[k, h], 0, 0, high)
                e[i, h] = e[i, h] - past if (i, h) in e else -past
    for k in range(NT):
        acc = dot(e[k, k], y[k], 0, 0, high)
        for j in range(k + 1, NT):
            acc = acc + dot(e[j, k], y[j], 0, 0, high)
        w_ref[k * TILE : (k + 1) * TILE, :] = acc
    share = factor_ref.shape[0]
    first = pl.multiple_of(blk_ref[0, 0] * share, 8)
    factor_ref[...] = u_ref[pl.ds(first, share), :] * (1.0 / 128.0)
    coef_ref[...] = w_ref[pl.ds(first, share), :]
    wt = jnp.concatenate([w_ref[...], jnp.zeros((COLS, TILE - SENSORS), F32)], axis=1).T[:SENSORS]
    hi = wt.astype(BF16)
    rest = wt - hi.astype(F32)
    mid = rest.astype(BF16)
    low = (rest - mid.astype(F32)).astype(BF16)
    parts = dot(jnp.concatenate([hi, mid, low], axis=0), lagged_ref[...], 1, 0)
    fitted = parts[:SENSORS] + (parts[SENSORS : 2 * SENSORS] + parts[2 * SENSORS :])
    resid_ref[...] = x_ref[...].astype(F32) - fitted


def on_device(signal, lag_table, window_end):
    blks, grps = lax.axis_size("blk"), lax.axis_size("grp")
    blk, grp = lax.axis_index("blk"), lax.axis_index("grp")
    x = signal[0]
    order = lambda b, g: b * grps + g
    following = [
        (order(b, g), order(b + 1, g) if b + 1 < blks else order(0, g + 1))
        for b in range(blks)
        for g in range(grps)
        if b + 1 < blks or g + 1 < grps
    ]
    tail = lax.ppermute(x[:, ROWS - TILE :], ("blk", "grp"), following)
    lagged, packed, spare, until = pl.pallas_call(
        gram_kernel,
        out_shape=[
            jax.ShapeDtypeStruct((COLS, ROWS), BF16),
            jax.ShapeDtypeStruct((PACKED, TILE), F32),
            jax.ShapeDtypeStruct((SPARE, TILE), F32),
            jax.ShapeDtypeStruct((grps, TILE), F32),
        ],
        in_specs=[SMEM, SMEM, VMEM, VMEM, VMEM],
        out_specs=[VMEM, VMEM, VMEM, VMEM],
        compiler_params=pltpu.CompilerParams(vmem_limit_bytes=40 << 20),
    )(window_end, grp.reshape(1, 1), lag_table[None, :], tail, x)

    core, chips = 2, blks // 2
    column = [[z * core + c for z in range(chips)] for c in range(core)]
    other = [(i, i ^ 1) for i in range(blks)]
    c_index = blk % core

    def swap(part):
        return lax.all_to_all(part, "blk", 0, 0, axis_index_groups=column)

    share = PACKED // blks
    parts = packed.reshape(chips, core, share, TILE)
    mine = lax.dynamic_index_in_dim(parts, c_index, 1, keepdims=False)
    theirs = lax.dynamic_index_in_dim(parts, 1 - c_index, 1, keepdims=False)
    mine = mine + lax.ppermute(theirs, "blk", other)
    mine = jnp.concatenate([swap(mine).sum(0), spare], axis=0)
    groups = lax.all_to_all(jnp.broadcast_to(mine[None], (grps, *mine.shape)), "grp", 0, 0)
    mine = (groups * until[:, None, :]).sum(0)
    prefix = lax.all_gather(mine, "blk", axis=0, tiled=True)

    out_rows = COLS // blks
    factor, coef, resid = pl.pallas_call(
        fit_kernel,
        out_shape=[
            jax.ShapeDtypeStruct((out_rows, COLS), F32),
            jax.ShapeDtypeStruct((out_rows, SENSORS), F32),
            jax.ShapeDtypeStruct((SENSORS, ROWS), F32),
        ],
        in_specs=[SMEM, VMEM, VMEM, VMEM],
        out_specs=[VMEM, VMEM, VMEM],
        scratch_shapes=[
            pltpu.VMEM((COLS, COLS), F32),
            pltpu.VMEM((COLS, SENSORS), F32),
            pltpu.VMEM((160, TILE), F32),
        ],
        compiler_params=pltpu.CompilerParams(vmem_limit_bytes=40 << 20),
    )(blk.reshape(1, 1), prefix, lagged, x)
    return factor[None], coef[None], resid[None]


def solution(mesh):
    return jax.shard_map(
        on_device,
        mesh=mesh,
        in_specs=(P("grp", None, "blk"), P(), P("grp", "blk")),
        out_specs=(P("grp", "blk", None), P("grp", "blk", None), P("grp", None, "blk")),
        check_vma=False,
    )
```

```python
import jax
import jax.numpy as jnp
from jax import lax
from jax.experimental import pallas as pl
from jax.experimental.pallas import tpu as pltpu
from jax.sharding import PartitionSpec as P

F32 = jnp.float32
BF16 = jnp.bfloat16
RIDGE = 4.0
SENSORS = 64
LAGS = 8
COLS = 512
ROWS = 512
TILE = 128
NT = COLS // TILE
TILES = [(k, j) for k in range(NT) for j in range(k + 1, NT)]
PACKED = (len(TILES) + NT // 2 + NT // 2) * TILE
SPARE = 8
VMEM = pl.BlockSpec(memory_space=pltpu.VMEM)
SMEM = pl.BlockSpec(memory_space=pltpu.SMEM)


def dot(a, b, ca, cb, precision=None):
    return lax.dot_general(
        a, b, (((ca,), (cb,)), ((), ())), precision=precision, preferred_element_type=F32
    )


def gram_kernel(end_ref, grp_ref, table_ref, tail_ref, x_ref, lagged_ref, packed_ref, spare_ref, until_ref):
    x = x_ref[...]
    ext = jnp.concatenate([tail_ref[...], x], axis=1).astype(F32)
    pieces = [pltpu.roll(ext, d, 1)[:, TILE:].astype(BF16) for d in range(1, LAGS + 1)]
    canonical = jnp.concatenate(pieces, axis=0)
    pair = lax.broadcasted_iota(jnp.int32, (COLS, COLS), 0)
    chosen = jnp.where(pair == table_ref[...], 1.0, 0.0).astype(BF16)
    lagged = dot(chosen, canonical, 0, 0).astype(BF16)
    lagged_ref[...] = lagged
    time = lax.broadcasted_iota(jnp.int32, (COLS, ROWS), 1)
    masked = jnp.where(time < end_ref[0, 0], lagged.astype(F32), 0.0).astype(BF16)
    row = lax.broadcasted_iota(jnp.int32, (TILE, TILE), 0)
    column = lax.broadcasted_iota(jnp.int32, (TILE, TILE), 1)
    spare_ref[...] = jnp.zeros_like(spare_ref)
    group = lax.broadcasted_iota(jnp.int32, until_ref.shape, 0)
    until_ref[...] = jnp.where(group <= grp_ref[0, 0], 1.0, 0.0)
    for k in range(NT):
        rows = masked[k * TILE : (k + 1) * TILE]
        block = dot(rows, lagged[k * TILE :], 1, 1)
        for j in range(k + 1, NT):
            n = TILES.index((k, j)) * TILE
            packed_ref[n : n + TILE, :] = block[:, (j - k) * TILE : (j - k + 1) * TILE]
        tile = block[:, :TILE] + jnp.where(row == column, RIDGE, 0.0)
        if k % 2 == 0:
            first = tile
        else:
            n = (len(TILES) + k // 2) * TILE
            packed_ref[n : n + TILE, :] = jnp.where(row <= column, first, tile)
            spare_ref[k // 2 : k // 2 + 1, :] = jnp.sum(
                jnp.where(row == column, tile, 0.0), axis=0, keepdims=True
            )
    cross = dot(masked, x, 1, 1)
    half = COLS // 2
    n = (len(TILES) + NT // 2) * TILE
    packed_ref[n:, :] = jnp.concatenate([cross[:half], cross[half:]], axis=1)


def factor_tile(d_rows, rows_ref):
    n = len(d_rows)
    lane = lax.broadcasted_iota(jnp.int32, (8, TILE), 1)
    sub = lax.broadcasted_iota(jnp.int32, (8, TILE), 0)
    m = list(d_rows)
    d, x = [], []

    def col(v, c):
        return jnp.broadcast_to(v[:, c : c + 1], (8, TILE))

    def less(v, a, b):
        t = [a[i] * b[i] for i in range(8)]
        return v - (((t[0] + t[1]) + (t[2] + t[3])) + ((t[4] + t[5]) + (t[6] + t[7])))

    for p in range(n):
        base = 8 * p
        pivot = (lane >= base) & (lane < base + 8)

        def rows_of(v, slot, count):
            at = 8 * (slot + 10 * (p % 2))
            rows_ref[at : at + 8, :] = v
            return [jnp.broadcast_to(rows_ref[at + i : at + i + 1, :], (8, TILE)) for i in range(count)]

        s = {}
        for j in range(8):
            for i, v in enumerate(rows_of(col(m[p], base + j), j, j + 1)):
                s[i, j] = v
        r = rows_of(jnp.where(pivot, jnp.where(lane == base + sub, 1.0, 0.0), m[p]), 8, 8)
        cols = {q: [col(m[q], base + j) for j in range(8)] for q in range(p + 1, n)}
        for q in range(p + 1, n):
            m[q] = jnp.where(pivot, 0.0, m[q])
        cn = list(cols[p + 1]) if p + 1 < n else []
        sets = [r, cn] if cn else [r]
        u, inv = {}, [None] * 8
        for k in range(0, 8, 2):
            one, off, two = s[k, k], s[k, k + 1], s[k + 1, k + 1]
            w0 = lax.rsqrt(one)
            w1 = lax.rsqrt((one * two - off * off) * one) * one
            inv[k], inv[k + 1] = w0, w1
            u[k, k + 1] = off * w0
            u[k, k] = one * w0
            u[k + 1, k + 1] = (two - u[k, k + 1] * u[k, k + 1]) * w1
            for j in range(k + 2, 8):
                u[k, j] = s[k, j] * w0
                u[k + 1, j] = (s[k + 1, j] - u[k, k + 1] * u[k, j]) * w1
            for i in range(k + 2, 8):
                for j in range(i, 8):
                    s[i, j] = (s[i, j] - u[k, i] * u[k, j]) - u[k + 1, i] * u[k + 1, j]
            for v in sets:
                v[k] = v[k] * w0
                v[k + 1] = (v[k + 1] - u[k, k + 1] * v[k]) * w1
                for i in range(k + 2, 8):
                    v[i] = (v[i] - u[k, i] * v[k]) - u[k + 1, i] * v[k + 1]
        if p + 1 < n:
            m[p + 1] = less(m[p + 1], cn, r)
        if p + 2 < n:
            z = list(r)
            for k in reversed(range(8)):
                z[k] = z[k] * inv[k]
                for i in range(k):
                    z[i] = z[i] - u[i, k] * z[k]
            for q in range(p + 2, n):
                m[q] = less(m[q], cols[q], z)
        both = r[0]
        for i in range(1, 8):
            both = jnp.where(sub == i, r[i], both)
        corner = jnp.zeros((8, TILE), F32)
        for j in range(8):
            v = u[0, j]
            for i in range(1, j + 1):
                v = jnp.where(sub == i, u[i, j], v)
            corner = jnp.where((lane == base + j) & (sub <= j), v, corner)
        d.append(jnp.where(lane >= base + 8, both, corner))
        x.append(jnp.where(lane < base + 8, both, 0.0))
    return d, x


def fit_kernel(blk_ref, packed_ref, lagged_ref, x_ref, factor_ref, coef_ref, resid_ref, u_ref, w_ref, rows_ref):
    high = lax.Precision.HIGHEST
    half = COLS // 2
    devices = COLS // factor_ref.shape[0]
    share = PACKED // devices
    pitch = share + SPARE

    def packed_rows(start):
        pieces, at = [], start
        while at < start + TILE:
            stop = min(start + TILE, (at // share + 1) * share)
            lo = (at // share) * pitch + at % share
            pieces.append(packed_ref[lo : lo + stop - at, :])
            at = stop
        return jnp.concatenate(pieces, axis=0)

    spare = packed_ref[share:pitch, :]
    for i in range(1, devices):
        spare = spare + packed_ref[i * pitch + share : (i + 1) * pitch, :]
    row = lax.broadcasted_iota(jnp.int32, (TILE, TILE), 0)
    column = lax.broadcasted_iota(jnp.int32, (TILE, TILE), 1)
    g = {kj: packed_rows(n * TILE) for n, kj in enumerate(TILES)}
    for k in range(0, NT, 2):
        both = packed_rows((len(TILES) + k // 2) * TILE)
        flipped = both.T
        diagonal = jnp.broadcast_to(spare[k // 2 : k // 2 + 1, :], (TILE, TILE))
        g[k, k] = jnp.where(row <= column, both, flipped)
        other = jnp.where(row > column, both, flipped)
        g[k + 1, k + 1] = jnp.where(row == column, diagonal, other)
    base = (len(TILES) + NT // 2) * TILE
    b = []
    for k in range(NT):
        lo = (k * TILE // half) * SENSORS
        b.append(packed_rows(base + (k * TILE) % half)[:, lo : lo + SENSORS])
    u_ref[...] = jnp.zeros_like(u_ref)
    y = []
    e = {}
    for k in range(NT):
        d, xi = factor_tile([g[k, k][8 * q : 8 * q + 8] for q in range(TILE // 8)], rows_ref)
        ukk = jnp.concatenate(d, axis=0)
        xkk = jnp.concatenate(xi, axis=0)
        u_ref[k * TILE : (k + 1) * TILE, k * TILE : (k + 1) * TILE] = ukk
        panel = {}
        e[k, k] = xkk
        for j in range(k + 1, NT):
            panel[j] = dot(xkk, g[k, j], 1, 0, high)
            if j == k + 1:
                g[j, j] = g[j, j] - dot(panel[j], panel[j], 0, 0, high)
            u_ref[k * TILE : (k + 1) * TILE, j * TILE : (j + 1) * TILE] = panel[j]
        y.append(dot(xkk, b[k], 1, 0, high))
        for i in range(k):
            e[k, i] = dot(xkk, e[k, i], 1, 0, high)
        for i in range(k + 1, NT):
            for j in range(i, NT):
                if (i, j) != (k + 1, k + 1):
                    g[i, j] = g[i, j] - dot(panel[i], panel[j], 0, 0, high)
            b[i] = b[i] - dot(panel[i], y[k], 0, 0, high)
            for h in range(k + 1):
                past = dot(panel[i], e[k, h], 0, 0, high)
                e[i, h] = e[i, h] - past if (i, h) in e else -past
    for k in range(NT):
        acc = dot(e[k, k], y[k], 0, 0, high)
        for j in range(k + 1, NT):
            acc = acc + dot(e[j, k], y[j], 0, 0, high)
        w_ref[k * TILE : (k + 1) * TILE, :] = acc
    share = factor_ref.shape[0]
    first = pl.multiple_of(blk_ref[0, 0] * share, 8)
    factor_ref[...] = u_ref[pl.ds(first, share), :] * (1.0 / 128.0)
    coef_ref[...] = w_ref[pl.ds(first, share), :]
    wt = jnp.concatenate([w_ref[...], jnp.zeros((COLS, TILE - SENSORS), F32)], axis=1).T[:SENSORS]
    hi = wt.astype(BF16)
    rest = wt - hi.astype(F32)
    mid = rest.astype(BF16)
    low = (rest - mid.astype(F32)).astype(BF16)
    parts = dot(jnp.concatenate([hi, mid, low], axis=0), lagged_ref[...], 1, 0)
    fitted = parts[:SENSORS] + (parts[SENSORS : 2 * SENSORS] + parts[2 * SENSORS :])
    resid_ref[...] = x_ref[...].astype(F32) - fitted


def on_device(signal, lag_table, window_end):
    blks, grps = lax.axis_size("blk"), lax.axis_size("grp")
    blk, grp = lax.axis_index("blk"), lax.axis_index("grp")
    x = signal[0]
    order = lambda b, g: b * grps + g
    following = [
        (order(b, g), order(b + 1, g) if b + 1 < blks else order(0, g + 1))
        for b in range(blks)
        for g in range(grps)
        if b + 1 < blks or g + 1 < grps
    ]
    tail = lax.ppermute(x[:, ROWS - TILE :], ("blk", "grp"), following)
    lagged, packed, spare, until = pl.pallas_call(
        gram_kernel,
        out_shape=[
            jax.ShapeDtypeStruct((COLS, ROWS), BF16),
            jax.ShapeDtypeStruct((PACKED, TILE), F32),
            jax.ShapeDtypeStruct((SPARE, TILE), F32),
            jax.ShapeDtypeStruct((grps, TILE), F32),
        ],
        in_specs=[SMEM, SMEM, VMEM, VMEM, VMEM],
        out_specs=[VMEM, VMEM, VMEM, VMEM],
        compiler_params=pltpu.CompilerParams(vmem_limit_bytes=40 << 20),
    )(window_end, grp.reshape(1, 1), lag_table[None, :], tail, x)

    core, chips = 2, blks // 2
    column = [[z * core + c for z in range(chips)] for c in range(core)]
    other = [(i, i ^ 1) for i in range(blks)]
    c_index = blk % core

    def swap(part):
        return lax.all_to_all(part, "blk", 0, 0, axis_index_groups=column)

    share = PACKED // blks
    parts = packed.reshape(chips, core, share, TILE)
    mine = lax.dynamic_index_in_dim(parts, c_index, 1, keepdims=False)
    theirs = lax.dynamic_index_in_dim(parts, 1 - c_index, 1, keepdims=False)
    mine = mine + lax.ppermute(theirs, "blk", other)
    mine = jnp.concatenate([swap(mine).sum(0), spare], axis=0)
    groups = lax.all_to_all(jnp.broadcast_to(mine[None], (grps, *mine.shape)), "grp", 0, 0)
    mine = (groups * until[:, None, :]).sum(0)
    prefix = lax.all_gather(mine, "blk", axis=0, tiled=True)

    out_rows = COLS // blks
    factor, coef, resid = pl.pallas_call(
        fit_kernel,
        out_shape=[
            jax.ShapeDtypeStruct((out_rows, COLS), F32),
            jax.ShapeDtypeStruct((out_rows, SENSORS), F32),
            jax.ShapeDtypeStruct((SENSORS, ROWS), F32),
        ],
        in_specs=[SMEM, VMEM, VMEM, VMEM],
        out_specs=[VMEM, VMEM, VMEM],
        scratch_shapes=[
            pltpu.VMEM((COLS, COLS), F32),
            pltpu.VMEM((COLS, SENSORS), F32),
            pltpu.VMEM((160, TILE), F32),
        ],
        compiler_params=pltpu.CompilerParams(vmem_limit_bytes=40 << 20),
    )(blk.reshape(1, 1), prefix, lagged, x)
    return factor[None], coef[None], resid[None]


def solution(mesh):
    return jax.shard_map(
        on_device,
        mesh=mesh,
        in_specs=(P("grp", None, "blk"), P(), P("grp", "blk")),
        out_specs=(P("grp", "blk", None), P("grp", "blk", None), P("grp", None, "blk")),
        check_vma=False,
    )
```

```python
import jax
import jax.numpy as jnp
from jax import lax
from jax.experimental import pallas as pl
from jax.experimental.pallas import tpu as pltpu
from jax.sharding import PartitionSpec as P

F32 = jnp.float32
BF16 = jnp.bfloat16
RIDGE = 4.0
SENSORS = 64
LAGS = 8
COLS = 512
ROWS = 512
TILE = 128
NT = COLS // TILE
TILES = [(k, j) for k in range(NT) for j in range(k + 1, NT)]
PACKED = (len(TILES) + NT // 2 + NT // 2) * TILE
SPARE = 8
VMEM = pl.BlockSpec(memory_space=pltpu.VMEM)
SMEM = pl.BlockSpec(memory_space=pltpu.SMEM)


def dot(a, b, ca, cb, precision=None):
    return lax.dot_general(
        a, b, (((ca,), (cb,)), ((), ())), precision=precision, preferred_element_type=F32
    )


def gram_kernel(end_ref, grp_ref, table_ref, tail_ref, x_ref, lagged_ref, packed_ref, spare_ref, until_ref):
    x = x_ref[...]
    ext = jnp.concatenate([tail_ref[...], x], axis=1).astype(F32)
    pieces = [pltpu.roll(ext, d, 1)[:, TILE:].astype(BF16) for d in range(1, LAGS + 1)]
    canonical = jnp.concatenate(pieces, axis=0)
    pair = lax.broadcasted_iota(jnp.int32, (COLS, COLS), 0)
    chosen = jnp.where(pair == table_ref[...], 1.0, 0.0).astype(BF16)
    lagged = dot(chosen, canonical, 0, 0).astype(BF16)
    lagged_ref[...] = lagged
    time = lax.broadcasted_iota(jnp.int32, (COLS, ROWS), 1)
    masked = jnp.where(time < end_ref[0, 0], lagged.astype(F32), 0.0).astype(BF16)
    row = lax.broadcasted_iota(jnp.int32, (TILE, TILE), 0)
    column = lax.broadcasted_iota(jnp.int32, (TILE, TILE), 1)
    spare_ref[...] = jnp.zeros_like(spare_ref)
    group = lax.broadcasted_iota(jnp.int32, until_ref.shape, 0)
    until_ref[...] = jnp.where(group <= grp_ref[0, 0], 1.0, 0.0)
    for k in range(NT):
        rows = masked[k * TILE : (k + 1) * TILE]
        block = dot(rows, lagged[k * TILE :], 1, 1)
        for j in range(k + 1, NT):
            n = TILES.index((k, j)) * TILE
            packed_ref[n : n + TILE, :] = block[:, (j - k) * TILE : (j - k + 1) * TILE]
        tile = block[:, :TILE] + jnp.where(row == column, RIDGE, 0.0)
        if k % 2 == 0:
            first = tile
        else:
            n = (len(TILES) + k // 2) * TILE
            packed_ref[n : n + TILE, :] = jnp.where(row <= column, first, tile)
            spare_ref[k // 2 : k // 2 + 1, :] = jnp.sum(
                jnp.where(row == column, tile, 0.0), axis=0, keepdims=True
            )
    cross = dot(masked, x, 1, 1)
    half = COLS // 2
    n = (len(TILES) + NT // 2) * TILE
    packed_ref[n:, :] = jnp.concatenate([cross[:half], cross[half:]], axis=1)


def factor_tile(d_rows, rows_ref):
    n = len(d_rows)
    lane = lax.broadcasted_iota(jnp.int32, (8, TILE), 1)
    sub = lax.broadcasted_iota(jnp.int32, (8, TILE), 0)
    m = list(d_rows)
    d, x = [], []

    def col(v, c):
        return jnp.broadcast_to(v[:, c : c + 1], (8, TILE))

    def less(v, a, b):
        t = [a[i] * b[i] for i in range(8)]
        return v - (((t[0] + t[1]) + (t[2] + t[3])) + ((t[4] + t[5]) + (t[6] + t[7])))

    for p in range(n):
        base = 8 * p
        pivot = (lane >= base) & (lane < base + 8)

        def rows_of(v, slot, count):
            at = 8 * (slot + 10 * (p % 2))
            rows_ref[at : at + 8, :] = v
            return [jnp.broadcast_to(rows_ref[at + i : at + i + 1, :], (8, TILE)) for i in range(count)]

        s = {}
        for j in range(8):
            for i, v in enumerate(rows_of(col(m[p], base + j), j, j + 1)):
                s[i, j] = v
        r = rows_of(jnp.where(pivot, jnp.where(lane == base + sub, 1.0, 0.0), m[p]), 8, 8)
        cols = {q: [col(m[q], base + j) for j in range(8)] for q in range(p + 1, n)}
        for q in range(p + 1, n):
            m[q] = jnp.where(pivot, 0.0, m[q])
        cn = list(cols[p + 1]) if p + 1 < n else []
        sets = [r, cn] if cn else [r]
        u, inv = {}, [None] * 8
        for k in range(0, 8, 2):
            one, off, two = s[k, k], s[k, k + 1], s[k + 1, k + 1]
            w0 = lax.rsqrt(one)
            w1 = lax.rsqrt((one * two - off * off) * one) * one
            inv[k], inv[k + 1] = w0, w1
            u[k, k + 1] = off * w0
            u[k, k] = one * w0
            u[k + 1, k + 1] = (two - u[k, k + 1] * u[k, k + 1]) * w1
            for j in range(k + 2, 8):
                u[k, j] = s[k, j] * w0
                u[k + 1, j] = (s[k + 1, j] - u[k, k + 1] * u[k, j]) * w1
            for i in range(k + 2, 8):
                for j in range(i, 8):
                    s[i, j] = (s[i, j] - u[k, i] * u[k, j]) - u[k + 1, i] * u[k + 1, j]
            for v in sets:
                v[k] = v[k] * w0
                v[k + 1] = (v[k + 1] - u[k, k + 1] * v[k]) * w1
                for i in range(k + 2, 8):
                    v[i] = (v[i] - u[k, i] * v[k]) - u[k + 1, i] * v[k + 1]
        if p + 1 < n:
            m[p + 1] = less(m[p + 1], cn, r)
        if p + 2 < n:
            z = list(r)
            for k in reversed(range(8)):
                z[k] = z[k] * inv[k]
                for i in range(k):
                    z[i] = z[i] - u[i, k] * z[k]
            for q in range(p + 2, n):
                m[q] = less(m[q], cols[q], z)
        both = r[0]
        for i in range(1, 8):
            both = jnp.where(sub == i, r[i], both)
        corner = jnp.zeros((8, TILE), F32)
        for j in range(8):
            v = u[0, j]
            for i in range(1, j + 1):
                v = jnp.where(sub == i, u[i, j], v)
            corner = jnp.where((lane == base + j) & (sub <= j), v, corner)
        d.append(jnp.where(lane >= base + 8, both, corner))
        x.append(jnp.where(lane < base + 8, both, 0.0))
    return d, x


def fit_kernel(blk_ref, packed_ref, lagged_ref, x_ref, factor_ref, coef_ref, resid_ref, u_ref, w_ref, rows_ref):
    high = lax.Precision.HIGHEST
    half = COLS // 2
    devices = COLS // factor_ref.shape[0]
    share = PACKED // devices
    pitch = share + SPARE

    def packed_rows(start):
        pieces, at = [], start
        while at < start + TILE:
            stop = min(start + TILE, (at // share + 1) * share)
            lo = (at // share) * pitch + at % share
            pieces.append(packed_ref[lo : lo + stop - at, :])
            at = stop
        return jnp.concatenate(pieces, axis=0)

    spare = packed_ref[share:pitch, :]
    for i in range(1, devices):
        spare = spare + packed_ref[i * pitch + share : (i + 1) * pitch, :]
    row = lax.broadcasted_iota(jnp.int32, (TILE, TILE), 0)
    column = lax.broadcasted_iota(jnp.int32, (TILE, TILE), 1)
    g = {kj: packed_rows(n * TILE) for n, kj in enumerate(TILES)}
    for k in range(0, NT, 2):
        both = packed_rows((len(TILES) + k // 2) * TILE)
        flipped = both.T
        diagonal = jnp.broadcast_to(spare[k // 2 : k // 2 + 1, :], (TILE, TILE))
        g[k, k] = jnp.where(row <= column, both, flipped)
        other = jnp.where(row > column, both, flipped)
        g[k + 1, k + 1] = jnp.where(row == column, diagonal, other)
    base = (len(TILES) + NT // 2) * TILE
    b = []
    for k in range(NT):
        lo = (k * TILE // half) * SENSORS
        b.append(packed_rows(base + (k * TILE) % half)[:, lo : lo + SENSORS])
    u_ref[...] = jnp.zeros_like(u_ref)
    y = []
    e = {}
    for k in range(NT):
        d, xi = factor_tile([g[k, k][8 * q : 8 * q + 8] for q in range(TILE // 8)], rows_ref)
        ukk = jnp.concatenate(d, axis=0)
        xkk = jnp.concatenate(xi, axis=0)
        u_ref[k * TILE : (k + 1) * TILE, k * TILE : (k + 1) * TILE] = ukk
        panel = {}
        e[k, k] = xkk
        if k + 1 < NT:
            panel[k + 1] = dot(xkk, g[k, k + 1], 1, 0, high)
            g[k + 1, k + 1] = g[k + 1, k + 1] - dot(panel[k + 1], panel[k + 1], 0, 0, high)
        wide = [g[k, j] for j in range(k + 2, NT)] + [e[k, i] for i in range(k)] + [b[k]]
        solved = dot(xkk, jnp.concatenate(wide, axis=1), 1, 0, high)
        for n, j in enumerate(range(k + 2, NT)):
            panel[j] = solved[:, n * TILE : (n + 1) * TILE]
        at = max(NT - k - 2, 0)
        for i in range(k):
            e[k, i] = solved[:, (at + i) * TILE : (at + i + 1) * TILE]
        y.append(solved[:, (at + k) * TILE :])
        for j in range(k + 1, NT):
            u_ref[k * TILE : (k + 1) * TILE, j * TILE : (j + 1) * TILE] = panel[j]
        for i in range(k + 1, NT):
            js = [j for j in range(i, NT) if (i, j) != (k + 1, k + 1)]
            wide = [panel[j] for j in js] + [e[k, h] for h in range(k + 1)] + [y[k]]
            past = dot(panel[i], jnp.concatenate(wide, axis=1), 0, 0, high)
            for n, j in enumerate(js):
                g[i, j] = g[i, j] - past[:, n * TILE : (n + 1) * TILE]
            for h in range(k + 1):
                part = past[:, (len(js) + h) * TILE : (len(js) + h + 1) * TILE]
                e[i, h] = e[i, h] - part if (i, h) in e else -part
            b[i] = b[i] - past[:, (len(js) + k + 1) * TILE :]
    for k in range(NT):
        acc = dot(e[k, k], y[k], 0, 0, high)
        for j in range(k + 1, NT):
            acc = acc + dot(e[j, k], y[j], 0, 0, high)
        w_ref[k * TILE : (k + 1) * TILE, :] = acc
    share = factor_ref.shape[0]
    first = pl.multiple_of(blk_ref[0, 0] * share, 8)
    factor_ref[...] = u_ref[pl.ds(first, share), :] * (1.0 / 128.0)
    coef_ref[...] = w_ref[pl.ds(first, share), :]
    wt = jnp.concatenate([w_ref[...], jnp.zeros((COLS, TILE - SENSORS), F32)], axis=1).T[:SENSORS]
    hi = wt.astype(BF16)
    rest = wt - hi.astype(F32)
    mid = rest.astype(BF16)
    low = (rest - mid.astype(F32)).astype(BF16)
    parts = dot(jnp.concatenate([hi, mid, low], axis=0), lagged_ref[...], 1, 0)
    fitted = parts[:SENSORS] + (parts[SENSORS : 2 * SENSORS] + parts[2 * SENSORS :])
    resid_ref[...] = x_ref[...].astype(F32) - fitted


def on_device(signal, lag_table, window_end):
    blks, grps = lax.axis_size("blk"), lax.axis_size("grp")
    blk, grp = lax.axis_index("blk"), lax.axis_index("grp")
    x = signal[0]
    order = lambda b, g: b * grps + g
    following = [
        (order(b, g), order(b + 1, g) if b + 1 < blks else order(0, g + 1))
        for b in range(blks)
        for g in range(grps)
        if b + 1 < blks or g + 1 < grps
    ]
    tail = lax.ppermute(x[:, ROWS - TILE :], ("blk", "grp"), following)
    lagged, packed, spare, until = pl.pallas_call(
        gram_kernel,
        out_shape=[
            jax.ShapeDtypeStruct((COLS, ROWS), BF16),
            jax.ShapeDtypeStruct((PACKED, TILE), F32),
            jax.ShapeDtypeStruct((SPARE, TILE), F32),
            jax.ShapeDtypeStruct((grps, TILE), F32),
        ],
        in_specs=[SMEM, SMEM, VMEM, VMEM, VMEM],
        out_specs=[VMEM, VMEM, VMEM, VMEM],
        compiler_params=pltpu.CompilerParams(vmem_limit_bytes=40 << 20),
    )(window_end, grp.reshape(1, 1), lag_table[None, :], tail, x)

    core, chips = 2, blks // 2
    column = [[z * core + c for z in range(chips)] for c in range(core)]
    other = [(i, i ^ 1) for i in range(blks)]
    c_index = blk % core

    def swap(part):
        return lax.all_to_all(part, "blk", 0, 0, axis_index_groups=column)

    share = PACKED // blks
    parts = packed.reshape(chips, core, share, TILE)
    mine = lax.dynamic_index_in_dim(parts, c_index, 1, keepdims=False)
    theirs = lax.dynamic_index_in_dim(parts, 1 - c_index, 1, keepdims=False)
    mine = mine + lax.ppermute(theirs, "blk", other)
    mine = jnp.concatenate([swap(mine).sum(0), spare], axis=0)
    groups = lax.all_to_all(jnp.broadcast_to(mine[None], (grps, *mine.shape)), "grp", 0, 0)
    mine = (groups * until[:, None, :]).sum(0)
    prefix = lax.all_gather(mine, "blk", axis=0, tiled=True)

    out_rows = COLS // blks
    factor, coef, resid = pl.pallas_call(
        fit_kernel,
        out_shape=[
            jax.ShapeDtypeStruct((out_rows, COLS), F32),
            jax.ShapeDtypeStruct((out_rows, SENSORS), F32),
            jax.ShapeDtypeStruct((SENSORS, ROWS), F32),
        ],
        in_specs=[SMEM, VMEM, VMEM, VMEM],
        out_specs=[VMEM, VMEM, VMEM],
        scratch_shapes=[
            pltpu.VMEM((COLS, COLS), F32),
            pltpu.VMEM((COLS, SENSORS), F32),
            pltpu.VMEM((160, TILE), F32),
        ],
        compiler_params=pltpu.CompilerParams(vmem_limit_bytes=40 << 20),
    )(blk.reshape(1, 1), prefix, lagged, x)
    return factor[None], coef[None], resid[None]


def solution(mesh):
    return jax.shard_map(
        on_device,
        mesh=mesh,
        in_specs=(P("grp", None, "blk"), P(), P("grp", "blk")),
        out_specs=(P("grp", "blk", None), P("grp", "blk", None), P("grp", None, "blk")),
        check_vma=False,
    )
```
